128 devices in a mesh: rep: 2 (over core), space: 64 (over z, y, x).
Axes of the slice: x: 4, y: 4, z: 4, core: 2. Of those that a mesh axis runs over, the one named last changes fastest.
Arguments:
- particles: float32 [6, 2, 32768, 128], P(None, 'rep', 'space'), may hold values from -6 to 6
- pair_order: int32 [2, 32768, 128], P('rep', 'space'), may hold values from 0 to 127, each once within a row
- accepted: int32 [2, 32768, 64], P('rep', 'space'), may hold values 0 or 1
- direction: int32 [2, 32768, 64], P('rep', 'space'), may hold values from 0 to 255
- destination: int32 [2, 32768], P('rep', 'space'), may hold values from 0 to 63, as said below
- live_count: int32 [2, 64], P('rep', 'space'), may hold values from 256 to 512, as said below
- cell_index: int32 [2, 32768], P('rep', 'space'), may hold values from 0 to 255
Outputs:
- moved: float32 [6, 2, 49152, 128], P(None, 'rep', 'space')
- samples: float32 [4, 64, 256], P(None, 'space', 'rep')
The draws below stay inside these ranges and needn't reach their ends.
Inputs may be any that keep to these rules, and one draw needn't show every extreme that they name: Every block's destination is its own slab or one of the two beside it, slab 0 and slab 64 - 1 being beside each other; only live blocks leave; one slab of one replica sends at most 128 blocks to each of its two neighbours, and in every replica some slab sends exactly 128 to its upper and some slab exactly 128 to its lower neighbour. `live_count`: the count of live blocks of each slab of each replica; slab 0 of replica 0 is full.
All inputs are finite; a program needn't handle non-finite values. No bound on the sum of `accepted` on one device may be relied on, other than what follows from the above.
Results may differ from the reference program's by a relative error of at most 0.0003.
Values sent between devices are 32-bit elements; how exact they have to be, the bound alone decides.
No kernel may reach another device: no remote copies, remote signals or barrier semaphores. Data moves between devices by JAX's collectives and lax.ppermute only.
A program may use at most 64 MiB of HBM per device.

```python
import jax
import jax.numpy as jnp
from jax import lax

PART = 128
PAIRS = 64
NDIR = 256
CAP = 512
MOVE = 128
CELLS = 256
OUTCAP = 768
REPS = 2
SLABS = 64
BLOCKS = 32768


def migration_plan(key):
    count_key = jax.random.fold_in(key, 101)
    upper_key = jax.random.fold_in(key, 102)
    upper_full = jax.random.fold_in(key, 103)
    lower_key = jax.random.fold_in(key, 104)
    lower_full = jax.random.fold_in(key, 105)
    order_key = jax.random.fold_in(key, 106)
    slab_ids = jnp.arange(SLABS, dtype=jnp.int32)[None, :]
    replica_ids = jnp.arange(REPS, dtype=jnp.int32)[:, None]
    living = jax.random.randint(count_key, (REPS, SLABS), CAP // 2, CAP + 1)
    living = jnp.where((slab_ids == 0) & (replica_ids == 0), CAP, living)
    upward = jax.random.randint(upper_key, (REPS, SLABS), 0, MOVE + 1)
    upward = jnp.where(slab_ids == jax.random.randint(upper_full, (REPS, 1), 0, SLABS), MOVE, upward)
    downward = jax.random.randint(lower_key, (REPS, SLABS), 0, MOVE + 1)
    downward = jnp.where(slab_ids == jax.random.randint(lower_full, (REPS, 1), 0, SLABS), MOVE, downward)
    slots = jnp.arange(CAP, dtype=jnp.int32)[None, None, :]
    noise = jax.random.randint(order_key, (REPS, SLABS, CAP), 0, 2 ** 18)
    priority = noise * CAP + slots + jnp.where(slots < living[:, :, None], 0, 2 ** 30)
    ranking = jnp.argsort(jnp.argsort(priority, axis=-1), axis=-1)
    offset = jnp.where(ranking < upward[:, :, None], 1, jnp.where(ranking < (upward + downward)[:, :, None], SLABS - 1, 0))
    target = (slab_ids[:, :, None] + offset) % SLABS
    return (living.astype(jnp.int32), target.reshape(REPS, SLABS * CAP).astype(jnp.int32))


def draw_destination(key, part):
    return migration_plan(key)[1]


def draw_live_count(key, part):
    return migration_plan(key)[0]


def place_ends(values, own_key, smallest, largest):
    index_at = [jax.random.randint(jax.random.fold_in(own_key, axis), (), 0, length) for axis, length in enumerate(values.shape)]
    widest = values.shape.index(max(values.shape))
    beside = index_at[:widest] + [(index_at[widest] + 1) % values.shape[widest]] + index_at[widest + 1:]
    return values.at[tuple(index_at)].set(smallest).at[tuple(beside)].set(largest)


def block_scale(stream_key, shape, split, least, largest):
    def one(axis_at, shards_of):
        steps = jax.random.uniform(jax.random.fold_in(jax.random.fold_in(stream_key, 6), axis_at), (shards_of,), jnp.float32, least / len(split), largest / len(split))
        return jnp.repeat(jnp.exp(steps), shape[axis_at] // shards_of).reshape((-1,) + (1,) * (len(shape) - axis_at - 1))

    level = one(*split[0])
    for cut in split[1:]:
        level = level * one(*cut)
    return level


def bell_draw(key, shape, spread, most, pieces=(), held_as=jnp.bfloat16):
    factor_of = block_scale(key, shape, pieces, -0.22, 0.18) if pieces else 1.0
    array = jax.random.normal(key, shape, jnp.float32) * spread * factor_of
    return jnp.minimum(jnp.maximum(array, -most), most).astype(held_as)


def setup_inputs(seed: int = 0) -> dict:
    keys = jax.random.split(jax.random.key(seed), 8)
    return {
        "particles": bell_draw(keys[0], (6, REPS, BLOCKS, PART), 1.0, 6.0, ((1, 2), (2, 64)), jnp.float32),
        "pair_order": jax.vmap(lambda own: jax.random.permutation(own, PART))(jax.random.split(keys[1], REPS * BLOCKS)).reshape((REPS, BLOCKS, PART)).astype(jnp.int32),
        "accepted": place_ends((jax.random.randint(keys[2], (REPS, BLOCKS, PAIRS), 0, 2) < 1).astype(jnp.int32), jax.random.fold_in(keys[2], 1), 0, 1),
        "direction": place_ends(jax.random.randint(keys[3], (REPS, BLOCKS, PAIRS), 0, NDIR), jax.random.fold_in(keys[3], 1), 0, NDIR - 1).astype(jnp.int32),
        "destination": draw_destination(jax.random.fold_in(keys[7], 71), 0),
        "live_count": draw_live_count(jax.random.fold_in(keys[7], 71), 0),
        "cell_index": place_ends(jax.random.randint(keys[6], (REPS, BLOCKS), 0, CELLS), jax.random.fold_in(keys[6], 1), 0, CELLS - 1).astype(jnp.int32),
    }


time_step = 0.25
golden_turn = 2.399963229728653

def directions(index):
    turns = index.astype(jnp.float32)
    height = 1.0 - (2.0 * turns + 1.0) / NDIR
    radius = jnp.sqrt(1.0 - height * height)
    angle = turns * golden_turn
    return jnp.stack([radius * jnp.cos(angle), radius * jnp.sin(angle), height])

def place_block(values, order):
    return jnp.zeros_like(values).at[:, order].set(values)

def collide(velocity, pair_order, accepted, direction):
    permuted = jnp.take_along_axis(velocity, pair_order[None], axis=2)
    first = permuted[:, :, :PAIRS]
    second = permuted[:, :, PAIRS:]
    center = 0.5 * (first + second)
    relative = first - second
    speed = jnp.sqrt(lax.optimization_barrier(jnp.sum(relative * relative, axis=0)))
    unit = directions(direction)
    taken = (accepted == 1)[None]
    first_out = jnp.where(taken, center + 0.5 * speed * unit, first)
    second_out = jnp.where(taken, center - 0.5 * speed * unit, second)
    combined = jnp.concatenate([first_out, second_out], axis=2)
    return jax.vmap(place_block, in_axes=(1, 0), out_axes=1)(combined, pair_order)

def moments(velocity, living):
    sums = jnp.stack([lax.optimization_barrier(jnp.sum(velocity[0], axis=1)), lax.optimization_barrier(jnp.sum(velocity[1], axis=1)), lax.optimization_barrier(jnp.sum(velocity[2], axis=1)), lax.optimization_barrier(jnp.sum(lax.optimization_barrier(jnp.sum(velocity * velocity, axis=0)), axis=1))])
    return jnp.where(living[None], sums, 0.0)

def select_movers(updated, moving):
    ranking = jnp.cumsum(moving.astype(jnp.int32)) - 1
    slots = jnp.arange(MOVE, dtype=jnp.int32)
    matches = moving[None, :] & (ranking[None, :] == slots[:, None])
    sources = jnp.arange(moving.shape[0], dtype=jnp.int32)
    chosen = lax.optimization_barrier(jnp.sum(jnp.where(matches, sources[None, :], 0), axis=1)).astype(jnp.int32)
    is_valid = jnp.any(matches, axis=1)
    return jnp.where(is_valid[None, :, None], jnp.take(updated, chosen, axis=1), 0.0)

def one_replica(inputs):
    particles, pair_order, accepted, direction, destination, live_count, cell_index = inputs
    velocity = collide(particles[3:], pair_order, accepted, direction)
    position = particles[:3] + time_step * velocity
    updated = jnp.concatenate([position, velocity], axis=0)
    block_ids = jnp.arange(BLOCKS, dtype=jnp.int32)
    slot_index = block_ids % CAP
    slab_index = block_ids // CAP
    living = slot_index < live_count[slab_index]
    to_upper = living & (destination == (slab_index + 1) % SLABS)
    to_lower = living & (destination == (slab_index + SLABS - 1) % SLABS)
    staying = living & (destination == slab_index)
    term = moments(velocity, living)
    sampled = jax.ops.segment_sum(term.T, slab_index * CELLS + cell_index, num_segments=SLABS * CELLS)
    by_slab = updated.reshape(6, SLABS, CAP, PART)
    send_upper = jax.vmap(select_movers, in_axes=(1, 0), out_axes=1)(by_slab, to_upper.reshape(SLABS, CAP))
    send_lower = jax.vmap(select_movers, in_axes=(1, 0), out_axes=1)(by_slab, to_lower.reshape(SLABS, CAP))
    from_lower = jnp.roll(send_upper, 1, axis=1)
    from_upper = jnp.roll(send_lower, -1, axis=1)
    own_blocks = jnp.where(staying.reshape(SLABS, CAP)[None, :, :, None], by_slab, 0.0)
    moved = jnp.concatenate([from_lower, own_blocks, from_upper], axis=2).reshape(6, SLABS * OUTCAP, PART)
    return (moved, sampled.T)

def reference(particles, pair_order, accepted, direction, destination, live_count, cell_index):
    inputs = (jnp.moveaxis(particles, 1, 0), pair_order, accepted, direction, destination, live_count, cell_index)
    moved, sampled = lax.map(one_replica, inputs)
    moved = jnp.moveaxis(moved, 0, 1)
    samples = (lax.optimization_barrier(jnp.sum(sampled, axis=0)) / (PART * REPS)).reshape(4, SLABS, CELLS)
    return (moved, samples)
```

```python
import functools

import jax
import jax.numpy as jnp
import numpy as np
from jax import lax
from jax.experimental import pallas as pl
from jax.experimental.pallas import tpu as pltpu
from jax.sharding import PartitionSpec as P

PART = 128
PAIRS = 64
NDIR = 256
CAP = 512
MOVE = 128
CELLS = 256
OUTCAP = 768
SLABS = 64

time_step = 0.25
golden_turn = 2.399963229728653
TURN_HIGH = float(np.round(golden_turn / (2 * np.pi) * 4096) / 4096)
TURN_LOW = float(golden_turn / (2 * np.pi) - TURN_HIGH)

CONTRACT_LANES = (((1,), (1,)), ((), ()))


def fitted(function, powers):
    x = 0.25 * np.cos((np.arange(400) + 0.5) * np.pi / 400)
    basis = np.stack([x**p for p in powers], axis=1)
    return [float(c) for c in np.linalg.lstsq(basis, function(x), rcond=None)[0]]


SINE = fitted(lambda x: np.sin(2 * np.pi * x), [1, 3, 5, 7, 9])
COSINE = fitted(lambda x: np.cos(2 * np.pi * x), [0, 2, 4, 6, 8])


def polynomial(x, coefficients):
    total = jnp.full_like(x, coefficients[-1])
    for c in coefficients[-2::-1]:
        total = total * x + c
    return total


def directions(turns):
    height = 1.0 - (2.0 * turns + 1.0) * (1.0 / NDIR)
    radius = jnp.sqrt(1.0 - height * height)
    whole = turns * TURN_HIGH
    part = (whole - jnp.floor(whole + 0.5)) + turns * TURN_LOW
    fold = jnp.abs(part) - 0.25
    square = fold * fold
    cosine = -fold * polynomial(square, SINE)
    sine = polynomial(square, COSINE)
    sine = jnp.where(part < 0.0, -sine, sine)
    return radius * cosine, radius * sine, height


def swap_sublanes(x, distance):
    if distance == 4:
        return pltpu.roll(x, 4, 1)
    ahead = pltpu.roll(x, 8 - distance, 1)
    behind = pltpu.roll(x, distance, 1)
    low = (lax.broadcasted_iota(jnp.int32, x.shape, 1) & distance) == 0
    return jnp.where(low, ahead, behind)


def sort_rows(keys):
    n = keys.shape[-1]
    rows = [keys[8 * r : 8 * r + 8] for r in range(16)]
    sub = lax.broadcasted_iota(jnp.int32, (8, n), 0)

    def exchange(rows, bit, down_bit):
        new = list(rows)
        for r in range(16):
            other = r ^ (1 << bit)
            if r < other:
                small, large = jnp.minimum(rows[r], rows[other]), jnp.maximum(rows[r], rows[other])
                if down_bit is not None and (r >> down_bit) & 1:
                    small, large = large, small
                new[r], new[other] = small, large
        return new

    def exchange_sublanes(rows, distance):
        low = (sub & distance) == 0
        new = []
        for x in rows:
            y = swap_sublanes(x[None], distance)[0]
            new.append(jnp.where(low, jnp.minimum(x, y), jnp.maximum(x, y)))
        return new

    for stage in (1, 2, 3):
        for bit in range(stage - 1, -1, -1):
            rows = exchange(rows, bit, stage)
    for stage in (4, 5, 6, 7):
        flip = None
        if stage < 7:
            flip = jnp.where((sub & (1 << (stage - 4))) == 0, 1.0, -1.0)
            rows = [x * flip for x in rows]
        for bit in range(stage - 1, -1, -1):
            rows = exchange(rows, bit, None) if bit < 4 else exchange_sublanes(rows, 1 << (bit - 4))
        if flip is not None:
            rows = [x * flip for x in rows]
    return jnp.concatenate(rows, axis=0)


def partner_codes(order, info):
    taken = info > -0.5
    turns = jnp.maximum(info, 0.0)
    first, second = order[:PAIRS], order[PAIRS:]
    partner = jnp.concatenate([jnp.where(taken, second, first), jnp.where(taken, first, second)], axis=0)
    eighth = jnp.floor(order * 0.125)
    place = order * 16.0 - eighth * 127.0
    extra = jnp.concatenate([turns * 2.0, turns * 2.0 + 1.0], axis=0)
    return sort_rows(place * 65536.0 + partner * 512.0 + extra)


def collide(velocity, codes):
    partner = (codes >> 9) & 127
    turns = ((codes >> 1) & 255).astype(jnp.float32)
    other = [jnp.take_along_axis(v, partner, axis=1) for v in velocity]
    relative = [v - o for v, o in zip(velocity, other)]
    speed = jnp.sqrt(relative[0] * relative[0] + relative[1] * relative[1] + relative[2] * relative[2])
    half = 0.5 * speed
    half = jnp.where((codes & 1) == 0, half, -half)
    return [0.5 * (v + o) + half * u for v, o, u in zip(velocity, other, directions(turns))]


def split(x):
    high = x.astype(jnp.bfloat16)
    return high, (x - high.astype(jnp.float32)).astype(jnp.bfloat16)


def dot(a, b):
    return jnp.dot(a, b, preferred_element_type=jnp.float32)


def dot_lanes(a, b):
    return lax.dot_general(a, b, CONTRACT_LANES, preferred_element_type=jnp.float32)


def pick(selection, x):
    high, low = split(x)
    return dot(selection, high) + dot(selection, low)


def mover_selection(destination, live, target):
    slots = lax.broadcasted_iota(jnp.int32, (1, CAP), 1)
    moving = (slots < live) & (destination == target)
    ahead = lax.broadcasted_iota(jnp.int32, (CAP, CAP), 0) < lax.broadcasted_iota(jnp.int32, (CAP, CAP), 1)
    flags = jnp.broadcast_to(jnp.where(moving, 1.0, 0.0), (8, CAP))
    ranking = dot(flags.astype(jnp.bfloat16), jnp.where(ahead, 1.0, 0.0).astype(jnp.bfloat16))[:1]
    ranking = jnp.where(moving, ranking, -1.0)
    rows = lax.broadcasted_iota(jnp.int32, (MOVE, CAP), 0).astype(jnp.float32)
    return jnp.where(ranking == rows, 1.0, 0.0).astype(jnp.bfloat16)


def position_kernel(scalars, destination, position, out):
    selection = mover_selection(destination[...], scalars[0], scalars[1])
    for c in range(3):
        out[c] = pick(selection, position[c, 0])


def movers_collided(scalars, at, destination, velocity, order, accepted, direction):
    selection = mover_selection(destination[...], scalars[0], scalars[at])
    info = jnp.where(accepted[0] == 1, direction[0], -1).astype(jnp.float32).astype(jnp.bfloat16)
    chosen = dot_lanes(info, selection)
    orders = dot(selection, order[0].astype(jnp.float32).astype(jnp.bfloat16))
    codes = partner_codes(orders.T, chosen).T.astype(jnp.int32)
    return selection, collide([pick(selection, velocity[c, 0]) for c in range(3)], codes)


def upward_kernel(scalars, destination, velocity, order, accepted, direction, sent, out):
    del sent
    _, result = movers_collided(scalars, 1, destination, velocity, order, accepted, direction)
    for c in range(3):
        out[c] = result[c]


def downward_kernel(scalars, destination, particles, order, accepted, direction, sent, out):
    del sent
    velocity = particles.at[3:6]
    selection, result = movers_collided(scalars, 2, destination, velocity, order, accepted, direction)
    for c in range(3):
        out[3 + c] = result[c]
        out[c] = pick(selection, particles[c, 0]) + time_step * result[c]


def own_kernel(scalars, destination, cells, particles, order, accepted, direction, sent, moved, mine, theirs, total):
    del sent
    step = pl.program_id(0)
    slots = lax.broadcasted_iota(jnp.int32, (1, PART), 1) + step * PART
    live = slots < scalars[0]
    staying = jnp.where(live & (destination[...] == scalars[3]), 1.0, 0.0)
    info = jnp.where(accepted[0] == 1, direction[0], -1).astype(jnp.float32)
    codes = partner_codes(order[0].astype(jnp.float32).T, info) + staying * 8388608.0
    codes = codes.T.astype(jnp.int32)
    keep = (codes >> 23) == 1
    result = collide([particles[3 + c, 0] for c in range(3)], codes)
    for c in range(3):
        moved[3 + c, 0] = jnp.where(keep, result[c], 0.0)
        moved[c, 0] = jnp.where(keep, particles[c, 0] + time_step * result[c], 0.0)
    cell = (cells[...] + scalars[4] * (CELLS // 2)) & (CELLS - 1)
    cell = jnp.where(live, cell, -1)
    onehot = lax.broadcasted_iota(jnp.int32, (CELLS, PART), 0) == cell
    onehot = jnp.where(onehot, 1.0, 0.0).astype(jnp.bfloat16)
    squares = result[0] * result[0] + result[1] * result[1] + result[2] * result[2]
    for c, value in enumerate([*result, squares]):
        part = pick(onehot, value)

        @pl.when(step == 0)
        def _():
            total[c] = part

        @pl.when(step > 0)
        def _():
            total[c] += part

    @pl.when(step == CAP // PART - 1)
    def _():
        ones = jnp.ones((8, PART), jnp.bfloat16)
        for c in range(4):
            high, low = split(total[c])
            sums = dot_lanes(ones, high) + dot_lanes(ones, low)
            mine[c : c + 1] = sums[:1, : CELLS // 2]
            theirs[c : c + 1] = sums[:1, CELLS // 2 :]


def below_kernel(held, arrived, moved):
    del held
    moved[:, 0] = arrived[...]


def above_kernel(held, position, velocity, mine, arrived, moved, samples, *, parts):
    del held
    for c in range(3):
        v = velocity[c]
        moved[3 + c, 0] = v
        moved[c, 0] = position[c] + time_step * v
    samples[:, 0] = (mine[...] + arrived[...]) * (1.0 / (PART * parts))


def whole(shape, at=None):
    at = at or (0,) * len(shape)
    return pl.BlockSpec(shape, lambda *_: at)


SMEM = pl.BlockSpec(memory_space=pltpu.SMEM)
ANY = pl.BlockSpec(memory_space=pl.ANY)


def from_behind(value, axis, steps):
    count = lax.axis_size(axis)
    pairs = [(source, (source + steps) % count) for source in range(count)]
    return lax.ppermute(value, axis, pairs)


def per_device(particles, pair_order, accepted, direction, destination, live_count, cell_index):
    accepted = jnp.swapaxes(accepted, 1, 2)
    direction = jnp.swapaxes(direction, 1, 2)
    slab = lax.axis_index("space")
    total = lax.axis_size("space")
    rep = lax.axis_index("rep")
    parts = lax.axis_size("rep")
    scalars = jnp.stack([live_count[0, 0], (slab + 1) % total, (slab + total - 1) % total, slab, rep]).astype(jnp.int32)
    f32 = jnp.float32
    limit = pltpu.CompilerParams(vmem_limit_bytes=40 * 2**20)
    once = dict(grid=(1,), compiler_params=limit)

    def cost(microseconds):
        return pl.CostEstimate(flops=0, bytes_accessed=int(microseconds * 3.0e6), transcendentals=0)


    row = whole((1, CAP))
    up_position = pl.pallas_call(
        position_kernel,
        in_specs=[SMEM, row, whole((3, 1, CAP, PART))],
        out_specs=whole((3, MOVE, PART)),
        out_shape=jax.ShapeDtypeStruct((3, MOVE, PART), f32),
        cost_estimate=cost(1),
        **once,
    )(scalars, destination, particles)
    position_from_lower = from_behind(up_position, "space", 1)

    pair_specs = [whole((1, CAP, PART)), whole((1, PAIRS, CAP)), whole((1, PAIRS, CAP)), ANY]
    up_velocity = pl.pallas_call(
        upward_kernel,
        in_specs=[SMEM, row, whole((3, 1, CAP, PART), (1, 0, 0, 0)), *pair_specs],
        out_specs=whole((3, MOVE, PART)),
        out_shape=jax.ShapeDtypeStruct((3, MOVE, PART), f32),
        cost_estimate=cost(2),
        **once,
    )(scalars, destination, particles, pair_order, accepted, direction, up_position)
    velocity_from_lower = from_behind(up_velocity, "space", 1)

    down = pl.pallas_call(
        downward_kernel,
        in_specs=[SMEM, row, whole((6, 1, CAP, PART)), *pair_specs],
        out_specs=whole((6, MOVE, PART)),
        out_shape=jax.ShapeDtypeStruct((6, MOVE, PART), f32),
        cost_estimate=cost(2),
        **once,
    )(scalars, destination, particles, pair_order, accepted, direction, up_velocity)
    from_upper = from_behind(down, "space", -1)

    lanes = pl.BlockSpec((1, PART), lambda i: (0, i))
    pairs = pl.BlockSpec((1, PAIRS, PART), lambda i: (0, 0, i))
    half = jax.ShapeDtypeStruct((4, CELLS // 2), f32)
    moved, mine, theirs = pl.pallas_call(
        own_kernel,
        grid=(CAP // PART,),
        in_specs=[
            SMEM,
            lanes,
            lanes,
            pl.BlockSpec((6, 1, PART, PART), lambda i: (0, 0, i, 0)),
            pl.BlockSpec((1, PART, PART), lambda i: (0, i, 0)),
            pairs,
            pairs,
            ANY,
        ],
        out_specs=[
            pl.BlockSpec((6, 1, PART, PART), lambda i: (0, 0, i + 1, 0)),
            whole((4, CELLS // 2)),
            whole((4, CELLS // 2)),
        ],
        out_shape=[jax.ShapeDtypeStruct((6, 1, OUTCAP, PART), f32), half, half],
        scratch_shapes=[pltpu.VMEM((4, CELLS, PART), f32)],
        cost_estimate=cost(5),
        compiler_params=limit,
    )(scalars, destination, cell_index, particles, pair_order, accepted, direction, down)
    arrived = from_behind(theirs, "rep", 1)

    moved = pl.pallas_call(
        below_kernel,
        in_specs=[ANY, whole((6, MOVE, PART))],
        out_specs=whole((6, 1, MOVE, PART), (0, 0, 5, 0)),
        out_shape=jax.ShapeDtypeStruct(moved.shape, f32),
        input_output_aliases={0: 0},
        **once,
    )(moved, from_upper)
    moved, samples = pl.pallas_call(
        functools.partial(above_kernel, parts=parts),
        in_specs=[ANY, whole((3, MOVE, PART)), whole((3, MOVE, PART)), whole((4, CELLS // 2)), whole((4, CELLS // 2))],
        out_specs=[whole((6, 1, MOVE, PART)), whole((4, 1, CELLS // 2))],
        out_shape=[jax.ShapeDtypeStruct(moved.shape, f32), jax.ShapeDtypeStruct((4, 1, CELLS // 2), f32)],
        input_output_aliases={0: 0},
        **once,
    )(moved, position_from_lower, velocity_from_lower, mine, arrived)
    return (moved, samples)


def solution(mesh):
    return jax.shard_map(
        per_device,
        mesh=mesh,
        in_specs=(
            P(None, "rep", "space", None),
            P("rep", "space", None),
            P("rep", "space", None),
            P("rep", "space", None),
            P("rep", "space"),
            P("rep", "space"),
            P("rep", "space"),
        ),
        out_specs=(P(None, "rep", "space", None), P(None, "space", "rep")),
        check_vma=False,
    )
```

```python
import functools

import jax
import jax.numpy as jnp
import numpy as np
from jax import lax
from jax.experimental import pallas as pl
from jax.experimental.pallas import tpu as pltpu
from jax.sharding import PartitionSpec as P

PART = 128
PAIRS = 64
NDIR = 256
CAP = 512
MOVE = 128
CELLS = 256
OUTCAP = 768
SLABS = 64

time_step = 0.25
golden_turn = 2.399963229728653
TURN_HIGH = float(np.round(golden_turn / (2 * np.pi) * 4096) / 4096)
TURN_LOW = float(golden_turn / (2 * np.pi) - TURN_HIGH)

CONTRACT_LANES = (((1,), (1,)), ((), ()))


def fitted(function, powers):
    x = 0.25 * np.cos((np.arange(400) + 0.5) * np.pi / 400)
    basis = np.stack([x**p for p in powers], axis=1)
    return [float(c) for c in np.linalg.lstsq(basis, function(x), rcond=None)[0]]


SINE = fitted(lambda x: np.sin(2 * np.pi * x), [1, 3, 5, 7, 9])
COSINE = fitted(lambda x: np.cos(2 * np.pi * x), [0, 2, 4, 6, 8])


def polynomial(x, coefficients):
    total = jnp.full_like(x, coefficients[-1])
    for c in coefficients[-2::-1]:
        total = total * x + c
    return total


def directions(turns):
    height = 1.0 - (2.0 * turns + 1.0) * (1.0 / NDIR)
    radius = jnp.sqrt(1.0 - height * height)
    whole = turns * TURN_HIGH
    part = (whole - jnp.floor(whole + 0.5)) + turns * TURN_LOW
    fold = jnp.abs(part) - 0.25
    square = fold * fold
    cosine = -fold * polynomial(square, SINE)
    sine = polynomial(square, COSINE)
    sine = jnp.where(part < 0.0, -sine, sine)
    return radius * cosine, radius * sine, height


def swap_sublanes(x, distance):
    if distance == 4:
        return pltpu.roll(x, 4, 1)
    ahead = pltpu.roll(x, 8 - distance, 1)
    behind = pltpu.roll(x, distance, 1)
    low = (lax.broadcasted_iota(jnp.int32, x.shape, 1) & distance) == 0
    return jnp.where(low, ahead, behind)


def sort_rows(keys):
    n = keys.shape[-1]
    rows = [keys[8 * r : 8 * r + 8] for r in range(16)]
    sub = lax.broadcasted_iota(jnp.int32, (8, n), 0)

    def exchange(rows, bit, down_bit):
        new = list(rows)
        for r in range(16):
            other = r ^ (1 << bit)
            if r < other:
                small, large = jnp.minimum(rows[r], rows[other]), jnp.maximum(rows[r], rows[other])
                if down_bit is not None and (r >> down_bit) & 1:
                    small, large = large, small
                new[r], new[other] = small, large
        return new

    def exchange_sublanes(rows, distance):
        low = (sub & distance) == 0
        new = []
        for x in rows:
            y = swap_sublanes(x[None], distance)[0]
            new.append(jnp.where(low, jnp.minimum(x, y), jnp.maximum(x, y)))
        return new

    for stage in (1, 2, 3):
        for bit in range(stage - 1, -1, -1):
            rows = exchange(rows, bit, stage)
    for stage in (4, 5, 6, 7):
        flip = None
        if stage < 7:
            flip = jnp.where((sub & (1 << (stage - 4))) == 0, 1.0, -1.0)
            rows = [x * flip for x in rows]
        for bit in range(stage - 1, -1, -1):
            rows = exchange(rows, bit, None) if bit < 4 else exchange_sublanes(rows, 1 << (bit - 4))
        if flip is not None:
            rows = [x * flip for x in rows]
    return jnp.concatenate(rows, axis=0)


def partner_codes(order, info):
    taken = info > -0.5
    turns = jnp.maximum(info, 0.0)
    first, second = order[:PAIRS], order[PAIRS:]
    partner = jnp.concatenate([jnp.where(taken, second, first), jnp.where(taken, first, second)], axis=0)
    eighth = jnp.floor(order * 0.125)
    place = order * 16.0 - eighth * 127.0
    extra = jnp.concatenate([turns * 2.0, turns * 2.0 + 1.0], axis=0)
    return sort_rows(place * 65536.0 + partner * 512.0 + extra)


def collide(velocity, codes):
    partner = (codes >> 9) & 127
    turns = ((codes >> 1) & 255).astype(jnp.float32)
    other = [jnp.take_along_axis(v, partner, axis=1) for v in velocity]
    relative = [v - o for v, o in zip(velocity, other)]
    speed = jnp.sqrt(relative[0] * relative[0] + relative[1] * relative[1] + relative[2] * relative[2])
    half = 0.5 * speed
    half = jnp.where((codes & 1) == 0, half, -half)
    return [0.5 * (v + o) + half * u for v, o, u in zip(velocity, other, directions(turns))]


def split(x):
    high = x.astype(jnp.bfloat16)
    return high, (x - high.astype(jnp.float32)).astype(jnp.bfloat16)


def dot(a, b):
    return jnp.dot(a, b, preferred_element_type=jnp.float32)


def dot_lanes(a, b):
    return lax.dot_general(a, b, CONTRACT_LANES, preferred_element_type=jnp.float32)


def pick(selection, x):
    high, low = split(x)
    return dot(selection, high) + dot(selection, low)


def mover_selection(destination, live, target):
    slots = lax.broadcasted_iota(jnp.int32, (1, CAP), 1)
    moving = (slots < live) & (destination == target)
    ahead = lax.broadcasted_iota(jnp.int32, (CAP, CAP), 0) < lax.broadcasted_iota(jnp.int32, (CAP, CAP), 1)
    flags = jnp.broadcast_to(jnp.where(moving, 1.0, 0.0), (8, CAP))
    ranking = dot(flags.astype(jnp.bfloat16), jnp.where(ahead, 1.0, 0.0).astype(jnp.bfloat16))[:1]
    ranking = jnp.where(moving, ranking, -1.0)
    rows = lax.broadcasted_iota(jnp.int32, (MOVE, CAP), 0).astype(jnp.float32)
    return jnp.where(ranking == rows, 1.0, 0.0).astype(jnp.bfloat16)


def place_on_mesh():
    return lax.axis_index("space"), lax.axis_index("rep")


def neighbour(steps):
    slab, _ = place_on_mesh()
    return lax.rem(slab + SLABS + steps, SLABS)


def movers_kernel(steps, live, destination, particles, order, accepted, direction, sent, out, data, orders, takens, turns, sems):
    del sent
    copies = [
        pltpu.make_async_copy(order, orders, sems.at[0]),
        pltpu.make_async_copy(accepted, takens, sems.at[1]),
        pltpu.make_async_copy(direction, turns, sems.at[2]),
        pltpu.make_async_copy(particles.at[3:6], data.at[3:6], sems.at[3]),
        pltpu.make_async_copy(particles.at[0:3], data.at[0:3], sems.at[4]),
    ]
    for c in copies:
        c.start()
    selection = mover_selection(destination[...], live[0, 0], neighbour(steps))
    for c in copies[:3]:
        c.wait()
    info = jnp.where(takens[0] == 1, turns[0], -1).astype(jnp.float32).astype(jnp.bfloat16)
    chosen = dot_lanes(info, selection)
    codes = partner_codes(dot(selection, orders[0].astype(jnp.float32).astype(jnp.bfloat16)).T, chosen)
    copies[3].wait()
    velocity = [pick(selection, data[3 + c, 0]) for c in range(3)]
    copies[4].wait()
    position = [pick(selection, data[c, 0]) for c in range(3)]
    result = collide(velocity, codes.T.astype(jnp.int32))
    for c in range(3):
        out[3 + c] = result[c]
        out[c] = position[c] + time_step * result[c]


def own_kernel(live_count, destination, cells, particles, order, accepted, direction, sent, moved, mine, theirs, total):
    del sent
    step = pl.program_id(0)
    slots = lax.broadcasted_iota(jnp.int32, (1, PART), 1) + step * PART
    slab, rep = place_on_mesh()
    live = slots < live_count[0, 0]
    staying = jnp.where(live & (destination[...] == slab), 1.0, 0.0)
    info = jnp.where(accepted[0] == 1, direction[0], -1).astype(jnp.float32)
    codes = partner_codes(order[0].astype(jnp.float32).T, info) + staying * 8388608.0
    codes = codes.T.astype(jnp.int32)
    keep = (codes >> 23) == 1
    result = collide([particles[3 + c, 0] for c in range(3)], codes)
    for c in range(3):
        moved[3 + c, 0] = jnp.where(keep, result[c], 0.0)
        moved[c, 0] = jnp.where(keep, particles[c, 0] + time_step * result[c], 0.0)
    cell = (cells[...] + rep * (CELLS // 2)) & (CELLS - 1)
    cell = jnp.where(live, cell, -1)
    onehot = lax.broadcasted_iota(jnp.int32, (CELLS, PART), 0) == cell
    onehot = jnp.where(onehot, 1.0, 0.0).astype(jnp.bfloat16)
    squares = result[0] * result[0] + result[1] * result[1] + result[2] * result[2]
    for c, value in enumerate([*result, squares]):
        part = pick(onehot, value)

        @pl.when(step == 0)
        def _():
            total[c] = part

        @pl.when(step > 0)
        def _():
            total[c] += part

    @pl.when(step == CAP // PART - 1)
    def _():
        ones = jnp.ones((8, PART), jnp.bfloat16)
        for c in range(4):
            high, low = split(total[c])
            sums = dot_lanes(ones, high) + dot_lanes(ones, low)
            mine[c : c + 1] = sums[:1, : CELLS // 2]
            theirs[c : c + 1] = sums[:1, CELLS // 2 :]


def below_kernel(held, arrived, moved):
    del held
    moved[:, 0] = arrived[...]


def above_kernel(parts, held, up, mine, arrived, moved, samples):
    del held
    moved[:, 0] = up[...]
    samples[:, 0] = (mine[...] + arrived[...]) * (1.0 / (PART * parts))


def whole(shape, at=None):
    at = at or (0,) * len(shape)
    return pl.BlockSpec(shape, lambda *_: at)


SMEM = pl.BlockSpec(memory_space=pltpu.SMEM)
ANY = pl.BlockSpec(memory_space=pl.ANY)


def from_behind(value, axis, steps):
    count = lax.axis_size(axis)
    pairs = [(source, (source + steps) % count) for source in range(count)]
    return lax.ppermute(value, axis, pairs)


def per_device(particles, pair_order, accepted, direction, destination, live_count, cell_index):
    accepted = jnp.swapaxes(accepted, 1, 2)
    direction = jnp.swapaxes(direction, 1, 2)
    parts = lax.axis_size("rep")
    f32 = jnp.float32
    limit = pltpu.CompilerParams(vmem_limit_bytes=56 * 2**20)
    once = dict(grid=(1,), compiler_params=limit)

    def movers(steps, after):
        return pl.pallas_call(
            functools.partial(movers_kernel, steps),
            in_specs=[SMEM, whole((1, CAP)), ANY, ANY, ANY, ANY, ANY],
            out_specs=whole((6, MOVE, PART)),
            out_shape=jax.ShapeDtypeStruct((6, MOVE, PART), f32),
            scratch_shapes=[
                pltpu.VMEM((6, 1, CAP, PART), f32),
                pltpu.VMEM((1, CAP, PART), jnp.int32),
                pltpu.VMEM((1, PAIRS, CAP), jnp.int32),
                pltpu.VMEM((1, PAIRS, CAP), jnp.int32),
                pltpu.SemaphoreType.DMA((5,)),
            ],
            **once,
        )(live_count, destination, particles, pair_order, accepted, direction, after)

    up = movers(1, live_count)
    from_lower = from_behind(up, "space", 1)

    lanes = pl.BlockSpec((1, PART), lambda i: (0, i))
    pairs = pl.BlockSpec((1, PAIRS, PART), lambda i: (0, 0, i))
    half = jax.ShapeDtypeStruct((4, CELLS // 2), f32)
    moved, mine, theirs = pl.pallas_call(
        own_kernel,
        grid=(CAP // PART,),
        in_specs=[
            SMEM,
            lanes,
            lanes,
            pl.BlockSpec((6, 1, PART, PART), lambda i: (0, 0, i, 0)),
            pl.BlockSpec((1, PART, PART), lambda i: (0, i, 0)),
            pairs,
            pairs,
            ANY,
        ],
        out_specs=[
            pl.BlockSpec((6, 1, PART, PART), lambda i: (0, 0, i + 1, 0)),
            whole((4, CELLS // 2)),
            whole((4, CELLS // 2)),
        ],
        out_shape=[jax.ShapeDtypeStruct((6, 1, OUTCAP, PART), f32), half, half],
        scratch_shapes=[pltpu.VMEM((4, CELLS, PART), f32)],
        compiler_params=limit,
    )(live_count, destination, cell_index, particles, pair_order, accepted, direction, up)
    arrived = from_behind(theirs, "rep", 1)
    from_upper = from_behind(movers(-1, mine), "space", -1)

    moved, samples = pl.pallas_call(
        functools.partial(above_kernel, parts),
        in_specs=[ANY, whole((6, MOVE, PART)), whole((4, CELLS // 2)), whole((4, CELLS // 2))],
        out_specs=[whole((6, 1, MOVE, PART)), whole((4, 1, CELLS // 2))],
        out_shape=[jax.ShapeDtypeStruct(moved.shape, f32), jax.ShapeDtypeStruct((4, 1, CELLS // 2), f32)],
        input_output_aliases={0: 0},
        grid=(1,),
        compiler_params=pltpu.CompilerParams(vmem_limit_bytes=8 * 2**20),
    )(moved, from_lower, mine, arrived)
    moved = pl.pallas_call(
        below_kernel,
        in_specs=[ANY, whole((6, MOVE, PART))],
        out_specs=whole((6, 1, MOVE, PART), (0, 0, 5, 0)),
        out_shape=jax.ShapeDtypeStruct(moved.shape, f32),
        input_output_aliases={0: 0},
        grid=(1,),
        compiler_params=pltpu.CompilerParams(vmem_limit_bytes=8 * 2**20),
    )(moved, from_upper)
    return (moved, samples)


def solution(mesh):
    return jax.shard_map(
        per_device,
        mesh=mesh,
        in_specs=(
            P(None, "rep", "space", None),
            P("rep", "space", None),
            P("rep", "space", None),
            P("rep", "space", None),
            P("rep", "space"),
            P("rep", "space"),
            P("rep", "space"),
        ),
        out_specs=(P(None, "rep", "space", None), P(None, "space", "rep")),
        check_vma=False,
    )
```

```python
import functools

import jax
import jax.numpy as jnp
import numpy as np
from jax import lax
from jax.experimental import pallas as pl
from jax.experimental.pallas import tpu as pltpu
from jax.sharding import PartitionSpec as P

PART = 128
PAIRS = 64
NDIR = 256
CAP = 512
MOVE = 128
CELLS = 256
OUTCAP = 768
SLABS = 64

time_step = 0.25
golden_turn = 2.399963229728653
TURN_HIGH = float(np.round(golden_turn / (2 * np.pi) * 4096) / 4096)
TURN_LOW = float(golden_turn / (2 * np.pi) - TURN_HIGH)

CONTRACT_LANES = (((1,), (1,)), ((), ()))


def fitted(function, powers):
    x = 0.25 * np.cos((np.arange(400) + 0.5) * np.pi / 400)
    basis = np.stack([x**p for p in powers], axis=1)
    return [float(c) for c in np.linalg.lstsq(basis, function(x), rcond=None)[0]]


SINE = fitted(lambda x: np.sin(2 * np.pi * x), [1, 3, 5, 7, 9])
COSINE = fitted(lambda x: np.cos(2 * np.pi * x), [0, 2, 4, 6, 8])


def polynomial(x, coefficients):
    total = jnp.full_like(x, coefficients[-1])
    for c in coefficients[-2::-1]:
        total = total * x + c
    return total


def directions(turns):
    height = 1.0 - (2.0 * turns + 1.0) * (1.0 / NDIR)
    radius = jnp.sqrt(1.0 - height * height)
    whole = turns * TURN_HIGH
    part = (whole - jnp.floor(whole + 0.5)) + turns * TURN_LOW
    fold = jnp.abs(part) - 0.25
    square = fold * fold
    cosine = -fold * polynomial(square, SINE)
    sine = polynomial(square, COSINE)
    sine = jnp.where(part < 0.0, -sine, sine)
    return radius * cosine, radius * sine, height


def swap_sublanes(x, distance):
    if distance == 4:
        return pltpu.roll(x, 4, 1)
    ahead = pltpu.roll(x, 8 - distance, 1)
    behind = pltpu.roll(x, distance, 1)
    low = (lax.broadcasted_iota(jnp.int32, x.shape, 1) & distance) == 0
    return jnp.where(low, ahead, behind)


def sort_rows(keys):
    n = keys.shape[-1]
    rows = [keys[8 * r : 8 * r + 8] for r in range(16)]
    sub = lax.broadcasted_iota(jnp.int32, (8, n), 0)

    def exchange(rows, bit, down_bit):
        new = list(rows)
        for r in range(16):
            other = r ^ (1 << bit)
            if r < other:
                small, large = jnp.minimum(rows[r], rows[other]), jnp.maximum(rows[r], rows[other])
                if down_bit is not None and (r >> down_bit) & 1:
                    small, large = large, small
                new[r], new[other] = small, large
        return new

    def exchange_sublanes(rows, distance):
        low = (sub & distance) == 0
        new = []
        for x in rows:
            y = swap_sublanes(x[None], distance)[0]
            new.append(jnp.where(low, jnp.minimum(x, y), jnp.maximum(x, y)))
        return new

    for stage in (1, 2, 3):
        for bit in range(stage - 1, -1, -1):
            rows = exchange(rows, bit, stage)
    for stage in (4, 5, 6, 7):
        flip = None
        if stage < 7:
            flip = jnp.where((sub & (1 << (stage - 4))) == 0, 1.0, -1.0)
            rows = [x * flip for x in rows]
        for bit in range(stage - 1, -1, -1):
            rows = exchange(rows, bit, None) if bit < 4 else exchange_sublanes(rows, 1 << (bit - 4))
        if flip is not None:
            rows = [x * flip for x in rows]
    return jnp.concatenate(rows, axis=0)


def partner_codes(order, info):
    taken = info > -0.5
    turns = jnp.maximum(info, 0.0)
    first, second = order[:PAIRS], order[PAIRS:]
    partner = jnp.concatenate([jnp.where(taken, second, first), jnp.where(taken, first, second)], axis=0)
    eighth = jnp.floor(order * 0.125)
    place = order * 16.0 - eighth * 127.0
    extra = jnp.concatenate([turns * 2.0, turns * 2.0 + 1.0], axis=0)
    return sort_rows(place * 65536.0 + partner * 512.0 + extra)


def collide(velocity, codes):
    partner = (codes >> 9) & 127
    turns = ((codes >> 1) & 255).astype(jnp.float32)
    other = [jnp.take_along_axis(v, partner, axis=1) for v in velocity]
    relative = [v - o for v, o in zip(velocity, other)]
    speed = jnp.sqrt(relative[0] * relative[0] + relative[1] * relative[1] + relative[2] * relative[2])
    half = 0.5 * speed
    half = jnp.where((codes & 1) == 0, half, -half)
    return [0.5 * (v + o) + half * u for v, o, u in zip(velocity, other, directions(turns))]


def split(x):
    high = x.astype(jnp.bfloat16)
    return high, (x - high.astype(jnp.float32)).astype(jnp.bfloat16)


def dot(a, b):
    return jnp.dot(a, b, preferred_element_type=jnp.float32)


def dot_lanes(a, b):
    return lax.dot_general(a, b, CONTRACT_LANES, preferred_element_type=jnp.float32)


def pick(selection, x):
    high, low = split(x)
    return dot(selection, high) + dot(selection, low)


def mover_selection(destination):
    up = destination == neighbour(1)
    down = destination == neighbour(-1)
    ahead = lax.broadcasted_iota(jnp.int32, (CAP, CAP), 0) < lax.broadcasted_iota(jnp.int32, (CAP, CAP), 1)
    flags = jnp.concatenate([jnp.where(up, 1.0, 0.0), jnp.where(down, 1.0, 0.0), jnp.zeros((6, CAP), jnp.float32)], axis=0)
    ranking = dot(flags.astype(jnp.bfloat16), jnp.where(ahead, 1.0, 0.0).astype(jnp.bfloat16))
    rows = lax.broadcasted_iota(jnp.int32, (MOVE, CAP), 0).astype(jnp.float32)
    chosen = [rows == jnp.where(moving, ranking[i : i + 1], -1.0) for i, moving in enumerate((up, down))]
    return jnp.where(jnp.concatenate(chosen, axis=0), 1.0, 0.0).astype(jnp.bfloat16)


def place_on_mesh():
    return lax.axis_index("space"), lax.axis_index("rep")


def neighbour(steps):
    slab, _ = place_on_mesh()
    return lax.rem(slab + SLABS + steps, SLABS)


def movers_kernel(
    destination, order, accepted, direction, particles, up, down, targets, orders, takens, turns, data, sems
):
    copies = [
        pltpu.make_async_copy(source, target, sems.at[i])
        for i, (source, target) in enumerate(
            (
                (destination, targets),
                (order, orders),
                (accepted, takens),
                (direction, turns),
                (particles.at[3:6], data.at[3:6]),
                (particles.at[0:3], data.at[0:3]),
            )
        )
    ]
    for c in copies:
        c.start()
    copies[0].wait()
    selection = mover_selection(targets[...])
    for c in copies[1:4]:
        c.wait()
    info = jnp.where(takens[0] == 1, turns[0], -1).astype(jnp.float32).astype(jnp.bfloat16)
    chosen = dot_lanes(info, selection)
    order_rows = dot(selection, orders[0].astype(jnp.float32).astype(jnp.bfloat16))
    codes = []
    for i in range(2):
        part = slice(i * MOVE, (i + 1) * MOVE)
        codes.append(partner_codes(order_rows[part].T, chosen[:, part]).T.astype(jnp.int32))
    copies[4].wait()
    velocity = [pick(selection, data[3 + c, 0]) for c in range(3)]
    copies[5].wait()
    position = [pick(selection, data[c, 0]) for c in range(3)]
    for i, out in enumerate((up, down)):
        part = slice(i * MOVE, (i + 1) * MOVE)
        result = collide([v[part] for v in velocity], codes[i])
        for c in range(3):
            out[3 + c] = result[c]
            out[c] = position[c][part] + time_step * result[c]


def own_kernel(live_count, destination, cells, particles, order, accepted, direction, sent, moved, mine, theirs, total):
    del sent
    step = pl.program_id(0)
    slots = lax.broadcasted_iota(jnp.int32, (1, PART), 1) + step * PART
    slab, rep = place_on_mesh()
    live = slots < live_count[0, 0]
    staying = jnp.where(live & (destination[...] == slab), 1.0, 0.0)
    info = jnp.where(accepted[0] == 1, direction[0], -1).astype(jnp.float32)
    codes = partner_codes(order[0].astype(jnp.float32).T, info) + staying * 8388608.0
    codes = codes.T.astype(jnp.int32)
    keep = (codes >> 23) == 1
    result = collide([particles[3 + c, 0] for c in range(3)], codes)
    for c in range(3):
        moved[3 + c, 0] = jnp.where(keep, result[c], 0.0)
        moved[c, 0] = jnp.where(keep, particles[c, 0] + time_step * result[c], 0.0)
    cell = (cells[...] + rep * (CELLS // 2)) & (CELLS - 1)
    cell = jnp.where(live, cell, -1)
    onehot = lax.broadcasted_iota(jnp.int32, (CELLS, PART), 0) == cell
    onehot = jnp.where(onehot, 1.0, 0.0).astype(jnp.bfloat16)
    squares = result[0] * result[0] + result[1] * result[1] + result[2] * result[2]
    for c, value in enumerate([*result, squares]):
        part = pick(onehot, value)

        @pl.when(step == 0)
        def _():
            total[c] = part

        @pl.when(step > 0)
        def _():
            total[c] += part

    @pl.when(step == CAP // PART - 1)
    def _():
        ones = jnp.ones((8, PART), jnp.bfloat16)
        for c in range(4):
            high, low = split(total[c])
            sums = dot_lanes(ones, high) + dot_lanes(ones, low)
            mine[c : c + 1] = sums[:1, : CELLS // 2]
            theirs[c : c + 1] = sums[:1, CELLS // 2 :]


def arrivals_kernel(parts, held, below, above, mine, arrived, moved, samples, sems):
    del held
    copies = [
        pltpu.make_async_copy(below, moved.at[:, 0, 0:MOVE], sems.at[0]),
        pltpu.make_async_copy(above, moved.at[:, 0, MOVE + CAP : OUTCAP], sems.at[1]),
    ]
    for c in copies:
        c.start()
    samples[:, 0] = (mine[...] + arrived[...]) * (1.0 / (PART * parts))
    for c in copies:
        c.wait()


def whole(shape, at=None):
    at = at or (0,) * len(shape)
    return pl.BlockSpec(shape, lambda *_: at)


SMEM = pl.BlockSpec(memory_space=pltpu.SMEM)
VMEM = pl.BlockSpec(memory_space=pltpu.VMEM)
HBM = pl.BlockSpec(memory_space=pltpu.HBM)


def from_behind(value, axis, steps):
    count = lax.axis_size(axis)
    pairs = [(source, (source + steps) % count) for source in range(count)]
    return lax.ppermute(value, axis, pairs)


def per_device(particles, pair_order, accepted, direction, destination, live_count, cell_index):
    accepted = jnp.swapaxes(accepted, 1, 2)
    direction = jnp.swapaxes(direction, 1, 2)
    parts = lax.axis_size("rep")
    f32 = jnp.float32
    limit = pltpu.CompilerParams(vmem_limit_bytes=56 * 2**20)

    sent = jax.ShapeDtypeStruct((6, MOVE, PART), f32)
    up, down = pl.pallas_call(
        movers_kernel,
        in_specs=[HBM] * 5,
        out_specs=[VMEM, VMEM],
        out_shape=[sent, sent],
        scratch_shapes=[
            pltpu.VMEM((1, CAP), jnp.int32),
            pltpu.VMEM((1, CAP, PART), jnp.int32),
            pltpu.VMEM((1, PAIRS, CAP), jnp.int32),
            pltpu.VMEM((1, PAIRS, CAP), jnp.int32),
            pltpu.VMEM((6, 1, CAP, PART), f32),
            pltpu.SemaphoreType.DMA((6,)),
        ],
        compiler_params=limit,
    )(destination, pair_order, accepted, direction, particles)
    from_lower = from_behind(up, "space", 1)
    from_upper = from_behind(down, "space", -1)

    lanes = pl.BlockSpec((1, PART), lambda i: (0, i))
    pairs = pl.BlockSpec((1, PAIRS, PART), lambda i: (0, 0, i))
    half = jax.ShapeDtypeStruct((4, CELLS // 2), f32)
    moved, mine, theirs = pl.pallas_call(
        own_kernel,
        grid=(CAP // PART,),
        in_specs=[
            SMEM,
            lanes,
            lanes,
            pl.BlockSpec((6, 1, PART, PART), lambda i: (0, 0, i, 0)),
            pl.BlockSpec((1, PART, PART), lambda i: (0, i, 0)),
            pairs,
            pairs,
            HBM,
        ],
        out_specs=[
            pl.BlockSpec((6, 1, PART, PART), lambda i: (0, 0, i + 1, 0)),
            whole((4, CELLS // 2)),
            whole((4, CELLS // 2)),
        ],
        out_shape=[jax.ShapeDtypeStruct((6, 1, OUTCAP, PART), f32), half, half],
        scratch_shapes=[pltpu.VMEM((4, CELLS, PART), f32)],
        compiler_params=limit,
    )(live_count, destination, cell_index, particles, pair_order, accepted, direction, up)
    arrived = from_behind(theirs, "rep", 1)
    moved, samples = pl.pallas_call(
        functools.partial(arrivals_kernel, parts),
        in_specs=[HBM, VMEM, VMEM, VMEM, VMEM],
        out_specs=[HBM, VMEM],
        out_shape=[jax.ShapeDtypeStruct(moved.shape, f32), jax.ShapeDtypeStruct((4, 1, CELLS // 2), f32)],
        input_output_aliases={0: 0},
        scratch_shapes=[pltpu.SemaphoreType.DMA((2,))],
        compiler_params=pltpu.CompilerParams(vmem_limit_bytes=8 * 2**20),
    )(moved, from_lower, from_upper, mine, arrived)
    return (moved, samples)


def solution(mesh):
    return jax.shard_map(
        per_device,
        mesh=mesh,
        in_specs=(
            P(None, "rep", "space", None),
            P("rep", "space", None),
            P("rep", "space", None),
            P("rep", "space", None),
            P("rep", "space"),
            P("rep", "space"),
            P("rep", "space"),
        ),
        out_specs=(P(None, "rep", "space", None), P(None, "space", "rep")),
        check_vma=False,
    )
```

```python
import functools

import jax
import jax.numpy as jnp
import numpy as np
from jax import lax
from jax.experimental import pallas as pl
from jax.experimental.pallas import tpu as pltpu
from jax.sharding import PartitionSpec as P

PART = 128
PAIRS = 64
NDIR = 256
CAP = 512
MOVE = 128
CELLS = 256
OUTCAP = 768
SLABS = 64

time_step = 0.25
golden_turn = 2.399963229728653
TURN_HIGH = float(np.round(golden_turn / (2 * np.pi) * 4096) / 4096)
TURN_LOW = float(golden_turn / (2 * np.pi) - TURN_HIGH)

CONTRACT_LANES = (((1,), (1,)), ((), ()))


def fitted(function, powers):
    x = 0.25 * np.cos((np.arange(400) + 0.5) * np.pi / 400)
    basis = np.stack([x**p for p in powers], axis=1)
    return [float(c) for c in np.linalg.lstsq(basis, function(x), rcond=None)[0]]


SINE = fitted(lambda x: np.sin(2 * np.pi * x), [1, 3, 5, 7, 9])
COSINE = fitted(lambda x: np.cos(2 * np.pi * x), [0, 2, 4, 6, 8])


def polynomial(x, coefficients):
    total = jnp.full_like(x, coefficients[-1])
    for c in coefficients[-2::-1]:
        total = total * x + c
    return total


def directions(turns):
    height = 1.0 - (2.0 * turns + 1.0) * (1.0 / NDIR)
    radius = jnp.sqrt(1.0 - height * height)
    whole = turns * TURN_HIGH
    part = (whole - jnp.floor(whole + 0.5)) + turns * TURN_LOW
    fold = jnp.abs(part) - 0.25
    square = fold * fold
    cosine = -fold * polynomial(square, SINE)
    sine = polynomial(square, COSINE)
    sine = jnp.where(part < 0.0, -sine, sine)
    return radius * cosine, radius * sine, height


def swap_sublanes(x, distance):
    if distance == 4:
        return pltpu.roll(x, 4, 1)
    ahead = pltpu.roll(x, 8 - distance, 1)
    behind = pltpu.roll(x, distance, 1)
    low = (lax.broadcasted_iota(jnp.int32, x.shape, 1) & distance) == 0
    return jnp.where(low, ahead, behind)


def sort_rows(keys):
    n = keys.shape[-1]
    rows = [keys[8 * r : 8 * r + 8] for r in range(16)]
    sub = lax.broadcasted_iota(jnp.int32, (8, n), 0)

    def exchange(rows, bit, down_bit):
        new = list(rows)
        for r in range(16):
            other = r ^ (1 << bit)
            if r < other:
                small, large = jnp.minimum(rows[r], rows[other]), jnp.maximum(rows[r], rows[other])
                if down_bit is not None and (r >> down_bit) & 1:
                    small, large = large, small
                new[r], new[other] = small, large
        return new

    def exchange_sublanes(rows, distance):
        low = (sub & distance) == 0
        new = []
        for x in rows:
            y = swap_sublanes(x[None], distance)[0]
            new.append(jnp.where(low, jnp.minimum(x, y), jnp.maximum(x, y)))
        return new

    for stage in (1, 2, 3):
        for bit in range(stage - 1, -1, -1):
            rows = exchange(rows, bit, stage)
    for stage in (4, 5, 6, 7):
        flip = None
        if stage < 7:
            flip = jnp.where((sub & (1 << (stage - 4))) == 0, 1.0, -1.0)
            rows = [x * flip for x in rows]
        for bit in range(stage - 1, -1, -1):
            rows = exchange(rows, bit, None) if bit < 4 else exchange_sublanes(rows, 1 << (bit - 4))
        if flip is not None:
            rows = [x * flip for x in rows]
    return jnp.concatenate(rows, axis=0)


def partner_codes(order, info):
    taken = info > -0.5
    turns = jnp.maximum(info, 0.0)
    first, second = order[:PAIRS], order[PAIRS:]
    partner = jnp.concatenate([jnp.where(taken, second, first), jnp.where(taken, first, second)], axis=0)
    eighth = jnp.floor(order * 0.125)
    place = order * 16.0 - eighth * 127.0
    extra = jnp.concatenate([turns * 2.0, turns * 2.0 + 1.0], axis=0)
    return sort_rows(place * 65536.0 + partner * 512.0 + extra)


def collide(velocity, codes):
    partner = (codes >> 9) & 127
    turns = ((codes >> 1) & 255).astype(jnp.float32)
    other = [jnp.take_along_axis(v, partner, axis=1) for v in velocity]
    relative = [v - o for v, o in zip(velocity, other)]
    speed = jnp.sqrt(relative[0] * relative[0] + relative[1] * relative[1] + relative[2] * relative[2])
    half = 0.5 * speed
    half = jnp.where((codes & 1) == 0, half, -half)
    return [0.5 * (v + o) + half * u for v, o, u in zip(velocity, other, directions(turns))]


def split(x):
    high = x.astype(jnp.bfloat16)
    return high, (x - high.astype(jnp.float32)).astype(jnp.bfloat16)


def dot(a, b):
    return jnp.dot(a, b, preferred_element_type=jnp.float32)


def dot_lanes(a, b):
    return lax.dot_general(a, b, CONTRACT_LANES, preferred_element_type=jnp.float32)


def pick(selection, x):
    high, low = split(x)
    return dot(selection, high) + dot(selection, low)


def mover_selection(destination):
    up = destination == neighbour(1)
    down = destination == neighbour(-1)
    ahead = lax.broadcasted_iota(jnp.int32, (CAP, CAP), 0) < lax.broadcasted_iota(jnp.int32, (CAP, CAP), 1)
    flags = jnp.concatenate([jnp.where(up, 1.0, 0.0), jnp.where(down, 1.0, 0.0), jnp.zeros((6, CAP), jnp.float32)], axis=0)
    ranking = dot(flags.astype(jnp.bfloat16), jnp.where(ahead, 1.0, 0.0).astype(jnp.bfloat16))
    rows = lax.broadcasted_iota(jnp.int32, (MOVE, CAP), 0).astype(jnp.float32)
    chosen = [rows == jnp.where(moving, ranking[i : i + 1], -1.0) for i, moving in enumerate((up, down))]
    return jnp.where(jnp.concatenate(chosen, axis=0), 1.0, 0.0).astype(jnp.bfloat16)


def place_on_mesh():
    return lax.axis_index("space"), lax.axis_index("rep")


def neighbour(steps):
    slab, _ = place_on_mesh()
    return lax.rem(slab + SLABS + steps, SLABS)


def movers_kernel(
    destination, order, accepted, direction, particles, up, down, targets, orders, takens, turns, data, sems
):
    copies = [
        pltpu.make_async_copy(source, target, sems.at[i])
        for i, (source, target) in enumerate(
            (
                (destination, targets),
                (order, orders),
                (accepted, takens),
                (direction, turns),
                (particles.at[3:6], data.at[3:6]),
                (particles.at[0:3], data.at[0:3]),
            )
        )
    ]
    for c in copies:
        c.start()
    copies[0].wait()
    selection = mover_selection(targets[...])
    for c in copies[1:4]:
        c.wait()
    info = jnp.where(takens[0] == 1, turns[0], -1).astype(jnp.float32).astype(jnp.bfloat16)
    chosen = dot_lanes(info, selection)
    order_rows = dot(selection, orders[0].astype(jnp.float32).astype(jnp.bfloat16))
    codes = []
    for i in range(2):
        part = slice(i * MOVE, (i + 1) * MOVE)
        codes.append(partner_codes(order_rows[part].T, chosen[:, part]).T.astype(jnp.int32))
    copies[4].wait()
    velocity = [pick(selection, data[3 + c, 0]) for c in range(3)]
    copies[5].wait()
    position = [pick(selection, data[c, 0]) for c in range(3)]
    for i, out in enumerate((up, down)):
        part = slice(i * MOVE, (i + 1) * MOVE)
        result = collide([v[part] for v in velocity], codes[i])
        for c in range(3):
            out[3 + c] = result[c]
            out[c] = position[c][part] + time_step * result[c]


def own_kernel(live_count, destination, cells, particles, order, accepted, direction, sent, moved, mine, theirs, total):
    del sent
    step = pl.program_id(0)
    slots = lax.broadcasted_iota(jnp.int32, (1, PART), 1) + step * PART
    slab, rep = place_on_mesh()
    live = slots < live_count[0, 0]
    staying = jnp.where(live & (destination[...] == slab), 1.0, 0.0)
    info = jnp.where(accepted[0] == 1, direction[0], -1).astype(jnp.float32)
    codes = partner_codes(order[0].astype(jnp.float32).T, info) + staying * 8388608.0
    codes = codes.T.astype(jnp.int32)
    keep = (codes >> 23) == 1
    result = collide([particles[3 + c, 0] for c in range(3)], codes)
    for c in range(3):
        moved[3 + c, 0] = jnp.where(keep, result[c], 0.0)
        moved[c, 0] = jnp.where(keep, particles[c, 0] + time_step * result[c], 0.0)
    cell = (cells[...] + rep * (CELLS // 2)) & (CELLS - 1)
    cell = jnp.where(live, cell, -1)
    onehot = lax.broadcasted_iota(jnp.int32, (CELLS, PART), 0) == cell
    onehot = jnp.where(onehot, 1.0, 0.0).astype(jnp.bfloat16)
    squares = result[0] * result[0] + result[1] * result[1] + result[2] * result[2]
    ones = jnp.ones((8, PART), jnp.bfloat16)
    sums = []
    for value in [*result, squares]:
        high, low = split(value)
        sums.append((dot_lanes(ones, high) + dot_lanes(ones, low))[:1])
    high, low = split(jnp.concatenate(sums + [jnp.zeros((4, PART), jnp.float32)], axis=0))
    part = dot_lanes(high, onehot) + dot_lanes(low, onehot)

    @pl.when(step == 0)
    def _():
        total[...] = part

    @pl.when(step > 0)
    def _():
        total[...] += part

    @pl.when(step == CAP // PART - 1)
    def _():
        mine[...] = total[:4, : CELLS // 2]
        theirs[...] = total[:4, CELLS // 2 :]


def samples_kernel(parts, mine, arrived, samples):
    samples[:, 0] = (mine[...] + arrived[...]) * (1.0 / (PART * parts))


def arrivals_kernel(held, ready, below, above, moved, samples, sems):
    del held, ready, samples
    copies = [
        pltpu.make_async_copy(below, moved.at[:, 0, 0:MOVE], sems.at[0]),
        pltpu.make_async_copy(above, moved.at[:, 0, MOVE + CAP : OUTCAP], sems.at[1]),
    ]
    for c in copies:
        c.start()
    for c in copies:
        c.wait()


def whole(shape, at=None):
    at = at or (0,) * len(shape)
    return pl.BlockSpec(shape, lambda *_: at)


SMEM = pl.BlockSpec(memory_space=pltpu.SMEM)
VMEM = pl.BlockSpec(memory_space=pltpu.VMEM)
HBM = pl.BlockSpec(memory_space=pltpu.HBM)


def from_behind(value, axis, steps):
    count = lax.axis_size(axis)
    pairs = [(source, (source + steps) % count) for source in range(count)]
    return lax.ppermute(value, axis, pairs)


def per_device(particles, pair_order, accepted, direction, destination, live_count, cell_index):
    accepted = jnp.swapaxes(accepted, 1, 2)
    direction = jnp.swapaxes(direction, 1, 2)
    parts = lax.axis_size("rep")
    f32 = jnp.float32
    limit = pltpu.CompilerParams(vmem_limit_bytes=56 * 2**20)

    sent = jax.ShapeDtypeStruct((6, MOVE, PART), f32)
    up, down = pl.pallas_call(
        movers_kernel,
        in_specs=[HBM] * 5,
        out_specs=[VMEM, VMEM],
        out_shape=[sent, sent],
        scratch_shapes=[
            pltpu.VMEM((1, CAP), jnp.int32),
            pltpu.VMEM((1, CAP, PART), jnp.int32),
            pltpu.VMEM((1, PAIRS, CAP), jnp.int32),
            pltpu.VMEM((1, PAIRS, CAP), jnp.int32),
            pltpu.VMEM((6, 1, CAP, PART), f32),
            pltpu.SemaphoreType.DMA((6,)),
        ],
        compiler_params=limit,
    )(destination, pair_order, accepted, direction, particles)
    from_lower = from_behind(up, "space", 1)
    from_upper = from_behind(down, "space", -1)

    lanes = pl.BlockSpec((1, PART), lambda i: (0, i))
    pairs = pl.BlockSpec((1, PAIRS, PART), lambda i: (0, 0, i))
    half = jax.ShapeDtypeStruct((4, CELLS // 2), f32)
    moved, mine, theirs = pl.pallas_call(
        own_kernel,
        grid=(CAP // PART,),
        in_specs=[
            SMEM,
            lanes,
            lanes,
            pl.BlockSpec((6, 1, PART, PART), lambda i: (0, 0, i, 0)),
            pl.BlockSpec((1, PART, PART), lambda i: (0, i, 0)),
            pairs,
            pairs,
            HBM,
        ],
        out_specs=[
            pl.BlockSpec((6, 1, PART, PART), lambda i: (0, 0, i + 1, 0)),
            whole((4, CELLS // 2)),
            whole((4, CELLS // 2)),
        ],
        out_shape=[jax.ShapeDtypeStruct((6, 1, OUTCAP, PART), f32), half, half],
        scratch_shapes=[pltpu.VMEM((8, CELLS), f32)],
        compiler_params=limit,
    )(live_count, destination, cell_index, particles, pair_order, accepted, direction, down)
    arrived = from_behind(theirs, "rep", 1)
    small = pltpu.CompilerParams(vmem_limit_bytes=8 * 2**20)
    samples = pl.pallas_call(
        functools.partial(samples_kernel, parts),
        in_specs=[VMEM, VMEM],
        out_specs=VMEM,
        out_shape=jax.ShapeDtypeStruct((4, 1, CELLS // 2), f32),
        compiler_params=small,
    )(mine, arrived)
    moved, samples = pl.pallas_call(
        arrivals_kernel,
        in_specs=[HBM, HBM, VMEM, VMEM],
        out_specs=[HBM, HBM],
        out_shape=[jax.ShapeDtypeStruct(moved.shape, f32), jax.ShapeDtypeStruct(samples.shape, f32)],
        input_output_aliases={0: 0, 1: 1},
        scratch_shapes=[pltpu.SemaphoreType.DMA((2,))],
        compiler_params=small,
    )(moved, samples, from_lower, from_upper)
    return (moved, samples)


def solution(mesh):
    return jax.shard_map(
        per_device,
        mesh=mesh,
        in_specs=(
            P(None, "rep", "space", None),
            P("rep", "space", None),
            P("rep", "space", None),
            P("rep", "space", None),
            P("rep", "space"),
            P("rep", "space"),
            P("rep", "space"),
        ),
        out_specs=(P(None, "rep", "space", None), P(None, "space", "rep")),
        check_vma=False,
    )
```

```python
import functools

import jax
import jax.numpy as jnp
import numpy as np
from jax import lax
from jax.experimental import pallas as pl
from jax.experimental.pallas import tpu as pltpu
from jax.sharding import PartitionSpec as P

PART = 128
PAIRS = 64
NDIR = 256
CAP = 512
MOVE = 128
CELLS = 256
OUTCAP = 768
SLABS = 64

time_step = 0.25
golden_turn = 2.399963229728653
TURN_HIGH = float(np.round(golden_turn / (2 * np.pi) * 4096) / 4096)
TURN_LOW = float(golden_turn / (2 * np.pi) - TURN_HIGH)

CONTRACT_LANES = (((1,), (1,)), ((), ()))


def fitted(function, powers):
    x = 0.25 * np.cos((np.arange(400) + 0.5) * np.pi / 400)
    basis = np.stack([x**p for p in powers], axis=1)
    return [float(c) for c in np.linalg.lstsq(basis, function(x), rcond=None)[0]]


SINE = fitted(lambda x: np.sin(2 * np.pi * x), [1, 3, 5, 7, 9])
COSINE = fitted(lambda x: np.cos(2 * np.pi * x), [0, 2, 4, 6, 8])


def polynomial(x, coefficients):
    total = jnp.full_like(x, coefficients[-1])
    for c in coefficients[-2::-1]:
        total = total * x + c
    return total


def directions(turns):
    height = 1.0 - (2.0 * turns + 1.0) * (1.0 / NDIR)
    radius = jnp.sqrt(1.0 - height * height)
    whole = turns * TURN_HIGH
    part = (whole - jnp.floor(whole + 0.5)) + turns * TURN_LOW
    fold = jnp.abs(part) - 0.25
    square = fold * fold
    cosine = -fold * polynomial(square, SINE)
    sine = polynomial(square, COSINE)
    sine = jnp.where(part < 0.0, -sine, sine)
    return radius * cosine, radius * sine, height


def swap_sublanes(x, distance):
    if distance == 4:
        return pltpu.roll(x, 4, 1)
    ahead = pltpu.roll(x, 8 - distance, 1)
    behind = pltpu.roll(x, distance, 1)
    low = (lax.broadcasted_iota(jnp.int32, x.shape, 1) & distance) == 0
    return jnp.where(low, ahead, behind)


def sort_rows(keys):
    n = keys.shape[-1]
    rows = [keys[8 * r : 8 * r + 8] for r in range(16)]
    sub = lax.broadcasted_iota(jnp.int32, (8, n), 0)

    def exchange(rows, bit, down_bit):
        new = list(rows)
        for r in range(16):
            other = r ^ (1 << bit)
            if r < other:
                small, large = jnp.minimum(rows[r], rows[other]), jnp.maximum(rows[r], rows[other])
                if down_bit is not None and (r >> down_bit) & 1:
                    small, large = large, small
                new[r], new[other] = small, large
        return new

    def exchange_sublanes(rows, distance):
        low = (sub & distance) == 0
        new = []
        for x in rows:
            y = swap_sublanes(x[None], distance)[0]
            new.append(jnp.where(low, jnp.minimum(x, y), jnp.maximum(x, y)))
        return new

    for stage in (1, 2, 3):
        for bit in range(stage - 1, -1, -1):
            rows = exchange(rows, bit, stage)
    for stage in (4, 5, 6, 7):
        flip = None
        if stage < 7:
            flip = jnp.where((sub & (1 << (stage - 4))) == 0, 1.0, -1.0)
            rows = [x * flip for x in rows]
        for bit in range(stage - 1, -1, -1):
            rows = exchange(rows, bit, None) if bit < 4 else exchange_sublanes(rows, 1 << (bit - 4))
        if flip is not None:
            rows = [x * flip for x in rows]
    return jnp.concatenate(rows, axis=0)


def partner_codes(order, info):
    taken = info > -0.5
    turns = jnp.maximum(info, 0.0)
    first, second = order[:PAIRS], order[PAIRS:]
    partner = jnp.concatenate([jnp.where(taken, second, first), jnp.where(taken, first, second)], axis=0)
    eighth = jnp.floor(order * 0.125)
    place = order * 16.0 - eighth * 127.0
    extra = jnp.concatenate([turns * 2.0, turns * 2.0 + 1.0], axis=0)
    return sort_rows(place * 65536.0 + partner * 512.0 + extra)


def collide(velocity, codes):
    partner = (codes >> 9) & 127
    turns = ((codes >> 1) & 255).astype(jnp.float32)
    other = [jnp.take_along_axis(v, partner, axis=1) for v in velocity]
    relative = [v - o for v, o in zip(velocity, other)]
    speed = jnp.sqrt(relative[0] * relative[0] + relative[1] * relative[1] + relative[2] * relative[2])
    half = 0.5 * speed
    half = jnp.where((codes & 1) == 0, half, -half)
    return [0.5 * (v + o) + half * u for v, o, u in zip(velocity, other, directions(turns))]


def split(x):
    high = x.astype(jnp.bfloat16)
    return high, (x - high.astype(jnp.float32)).astype(jnp.bfloat16)


def dot(a, b):
    return jnp.dot(a, b, preferred_element_type=jnp.float32)


def dot_lanes(a, b):
    return lax.dot_general(a, b, CONTRACT_LANES, preferred_element_type=jnp.float32)


def pick(selection, x):
    high, low = split(x)
    return dot(selection, high) + dot(selection, low)


def mover_selection(destination):
    up = destination == neighbour(1)
    down = destination == neighbour(-1)
    ahead = lax.broadcasted_iota(jnp.int32, (CAP, CAP), 0) < lax.broadcasted_iota(jnp.int32, (CAP, CAP), 1)
    flags = jnp.concatenate([jnp.where(up, 1.0, 0.0), jnp.where(down, 1.0, 0.0), jnp.zeros((6, CAP), jnp.float32)], axis=0)
    ranking = dot(flags.astype(jnp.bfloat16), jnp.where(ahead, 1.0, 0.0).astype(jnp.bfloat16))
    rows = lax.broadcasted_iota(jnp.int32, (MOVE, CAP), 0).astype(jnp.float32)
    chosen = [rows == jnp.where(moving, ranking[i : i + 1], -1.0) for i, moving in enumerate((up, down))]
    return jnp.where(jnp.concatenate(chosen, axis=0), 1.0, 0.0).astype(jnp.bfloat16)


def place_on_mesh():
    return lax.axis_index("space"), lax.axis_index("rep")


def neighbour(steps):
    slab, _ = place_on_mesh()
    return lax.rem(slab + SLABS + steps, SLABS)


def movers_kernel(
    destination, order, accepted, direction, particles, cell, up, down, targets, orders, takens, turns, data, cells, sems
):
    copies = [
        pltpu.make_async_copy(source, target, sems.at[i])
        for i, (source, target) in enumerate(
            (
                (destination, targets),
                (order, orders),
                (accepted, takens),
                (direction, turns),
                (particles.at[3:6], data.at[3:6]),
                (particles.at[0:3], data.at[0:3]),
                (cell, cells),
            )
        )
    ]
    for c in copies:
        c.start()
    copies[0].wait()
    selection = mover_selection(targets[...])
    for c in copies[1:4]:
        c.wait()
    info = jnp.where(takens[0] == 1, turns[0], -1).astype(jnp.float32).astype(jnp.bfloat16)
    chosen = dot_lanes(info, selection)
    order_rows = dot(selection, orders[0].astype(jnp.float32).astype(jnp.bfloat16))
    codes = []
    for i in range(2):
        part = slice(i * MOVE, (i + 1) * MOVE)
        codes.append(partner_codes(order_rows[part].T, chosen[:, part]).T.astype(jnp.int32))
    copies[4].wait()
    velocity = [pick(selection, data[3 + c, 0]) for c in range(3)]
    copies[5].wait()
    position = [pick(selection, data[c, 0]) for c in range(3)]
    for i, out in enumerate((up, down)):
        part = slice(i * MOVE, (i + 1) * MOVE)
        result = collide([v[part] for v in velocity], codes[i])
        for c in range(3):
            out[3 + c] = result[c]
            out[c] = position[c][part] + time_step * result[c]
    copies[6].wait()


def own_kernel(live_count, destination, order, accepted, direction, particles, cells, moved, mine, theirs, out, sems):
    slab, rep = place_on_mesh()
    live = lax.broadcasted_iota(jnp.int32, (1, CAP), 1) < live_count[0, 0]
    staying = jnp.where(live & (destination[...] == slab), 8388608.0, 0.0)
    cell = jnp.where(live, (cells[...] + rep * (CELLS // 2)) & (CELLS - 1), -1)
    ones = jnp.ones((8, PART), jnp.bfloat16)
    total = jnp.zeros((8, CELLS), jnp.float32)
    copies = []
    for i in range(CAP // PART):
        part = slice(i * PART, (i + 1) * PART)
        info = jnp.where(accepted[0, :, part] == 1, direction[0, :, part], -1).astype(jnp.float32)
        codes = partner_codes(order[0, part].astype(jnp.float32).T, info) + staying[:, part]
        codes = codes.T.astype(jnp.int32)
        keep = (codes >> 23) == 1
        result = collide([particles[3 + c, 0, part] for c in range(3)], codes)
        for c in range(3):
            out[3 + c, part] = jnp.where(keep, result[c], 0.0)
            out[c, part] = jnp.where(keep, particles[c, 0, part] + time_step * result[c], 0.0)
        copies.append(
            pltpu.make_async_copy(
                out.at[:, part], moved.at[:, 0, MOVE + i * PART : MOVE + (i + 1) * PART], sems.at[i]
            )
        )
        copies[i].start()
        onehot = lax.broadcasted_iota(jnp.int32, (CELLS, PART), 0) == cell[:, part]
        onehot = jnp.where(onehot, 1.0, 0.0).astype(jnp.bfloat16)
        squares = result[0] * result[0] + result[1] * result[1] + result[2] * result[2]
        sums = []
        for value in [*result, squares]:
            high, low = split(value)
            sums.append((dot_lanes(ones, high) + dot_lanes(ones, low))[:1])
        high, low = split(jnp.concatenate(sums + [jnp.zeros((4, PART), jnp.float32)], axis=0))
        total += dot_lanes(high, onehot) + dot_lanes(low, onehot)
    mine[...] = total[:4, : CELLS // 2]
    theirs[...] = total[:4, CELLS // 2 :]
    for c in copies:
        c.wait()


def arrivals_kernel(parts, held, below, above, mine, arrived, moved, samples, sums, sems):
    del held
    copies = [
        pltpu.make_async_copy(below, moved.at[:, 0, 0:MOVE], sems.at[0]),
        pltpu.make_async_copy(above, moved.at[:, 0, MOVE + CAP : OUTCAP], sems.at[1]),
        pltpu.make_async_copy(sums, samples, sems.at[2]),
    ]
    copies[0].start()
    copies[1].start()
    sums[:, 0] = (mine[...] + arrived[...]) * (1.0 / (PART * parts))
    copies[2].start()
    for c in copies:
        c.wait()


def whole(shape, at=None):
    at = at or (0,) * len(shape)
    return pl.BlockSpec(shape, lambda *_: at)


SMEM = pl.BlockSpec(memory_space=pltpu.SMEM)
VMEM = pl.BlockSpec(memory_space=pltpu.VMEM)
HBM = pl.BlockSpec(memory_space=pltpu.HBM)


def in_hbm(*arrays):
    return [pltpu.with_memory_space_constraint(a, pltpu.HBM) for a in arrays]


def from_behind(value, axis, steps):
    count = lax.axis_size(axis)
    pairs = [(source, (source + steps) % count) for source in range(count)]
    return lax.ppermute(value, axis, pairs)


def per_device(particles, pair_order, accepted, direction, destination, live_count, cell_index):
    accepted = jnp.swapaxes(accepted, 1, 2)
    direction = jnp.swapaxes(direction, 1, 2)
    parts = lax.axis_size("rep")
    f32 = jnp.float32
    limit = pltpu.CompilerParams(vmem_limit_bytes=32 * 2**20)

    sent = jax.ShapeDtypeStruct((6, MOVE, PART), f32)
    up, down, *held = pl.pallas_call(
        movers_kernel,
        in_specs=[HBM] * 6,
        out_specs=[VMEM] * 8,
        out_shape=[
            sent,
            sent,
            pltpu.VMEM((1, CAP), jnp.int32),
            pltpu.VMEM((1, CAP, PART), jnp.int32),
            pltpu.VMEM((1, PAIRS, CAP), jnp.int32),
            pltpu.VMEM((1, PAIRS, CAP), jnp.int32),
            pltpu.VMEM((6, 1, CAP, PART), f32),
            pltpu.VMEM((1, CAP), jnp.int32),
        ],
        scratch_shapes=[pltpu.SemaphoreType.DMA((7,))],
        compiler_params=limit,
    )(*in_hbm(destination, pair_order, accepted, direction, particles, cell_index))
    from_lower = from_behind(up, "space", 1)
    from_upper = from_behind(down, "space", -1)

    half = jax.ShapeDtypeStruct((4, CELLS // 2), f32)
    moved, mine, theirs = pl.pallas_call(
        own_kernel,
        in_specs=[SMEM] + [VMEM] * 6,
        out_specs=[HBM, VMEM, VMEM],
        out_shape=[jax.ShapeDtypeStruct((6, 1, OUTCAP, PART), f32), half, half],
        scratch_shapes=[pltpu.VMEM((6, CAP, PART), f32), pltpu.SemaphoreType.DMA((CAP // PART,))],
        compiler_params=limit,
    )(live_count, *held)
    arrived = from_behind(theirs, "rep", 1)
    moved, samples = pl.pallas_call(
        functools.partial(arrivals_kernel, parts),
        in_specs=[HBM, VMEM, VMEM, VMEM, VMEM],
        out_specs=[HBM, HBM],
        out_shape=[jax.ShapeDtypeStruct(moved.shape, f32), jax.ShapeDtypeStruct((4, 1, CELLS // 2), f32)],
        input_output_aliases={0: 0},
        scratch_shapes=[pltpu.VMEM((4, 1, CELLS // 2), f32), pltpu.SemaphoreType.DMA((3,))],
        compiler_params=pltpu.CompilerParams(vmem_limit_bytes=8 * 2**20),
    )(moved, from_lower, from_upper, mine, arrived)
    return (moved, samples)


def solution(mesh):
    return jax.shard_map(
        per_device,
        mesh=mesh,
        in_specs=(
            P(None, "rep", "space", None),
            P("rep", "space", None),
            P("rep", "space", None),
            P("rep", "space", None),
            P("rep", "space"),
            P("rep", "space"),
            P("rep", "space"),
        ),
        out_specs=(P(None, "rep", "space", None), P(None, "space", "rep")),
        check_vma=False,
    )
```

```python
import functools

import jax
import jax.numpy as jnp
import numpy as np
from jax import lax
from jax.experimental import pallas as pl
from jax.experimental.pallas import tpu as pltpu
from jax.sharding import PartitionSpec as P

PART = 128
PAIRS = 64
NDIR = 256
CAP = 512
MOVE = 128
CELLS = 256
OUTCAP = 768
SLABS = 64

time_step = 0.25
golden_turn = 2.399963229728653
TURN_HIGH = float(np.round(golden_turn / (2 * np.pi) * 4096) / 4096)
TURN_LOW = float(golden_turn / (2 * np.pi) - TURN_HIGH)

CONTRACT_LANES = (((1,), (1,)), ((), ()))


def fitted(function, powers):
    x = 0.25 * np.cos((np.arange(400) + 0.5) * np.pi / 400)
    basis = np.stack([x**p for p in powers], axis=1)
    return [float(c) for c in np.linalg.lstsq(basis, function(x), rcond=None)[0]]


SINE = fitted(lambda x: np.sin(2 * np.pi * x), [1, 3, 5, 7, 9])
COSINE = fitted(lambda x: np.cos(2 * np.pi * x), [0, 2, 4, 6, 8])


def polynomial(x, coefficients):
    total = jnp.full_like(x, coefficients[-1])
    for c in coefficients[-2::-1]:
        total = total * x + c
    return total


def directions(turns):
    height = 1.0 - (2.0 * turns + 1.0) * (1.0 / NDIR)
    radius = jnp.sqrt(1.0 - height * height)
    whole = turns * TURN_HIGH
    part = (whole - jnp.floor(whole + 0.5)) + turns * TURN_LOW
    fold = jnp.abs(part) - 0.25
    square = fold * fold
    cosine = -fold * polynomial(square, SINE)
    sine = polynomial(square, COSINE)
    sine = jnp.where(part < 0.0, -sine, sine)
    return radius * cosine, radius * sine, height


def swap_sublanes(x, distance):
    if distance == 4:
        return pltpu.roll(x, 4, 1)
    ahead = pltpu.roll(x, 8 - distance, 1)
    behind = pltpu.roll(x, distance, 1)
    low = (lax.broadcasted_iota(jnp.int32, x.shape, 1) & distance) == 0
    return jnp.where(low, ahead, behind)


def sort_rows(keys):
    n = keys.shape[-1]
    rows = [keys[8 * r : 8 * r + 8] for r in range(16)]
    sub = lax.broadcasted_iota(jnp.int32, (8, n), 0)

    def exchange(rows, bit, down_bit):
        new = list(rows)
        for r in range(16):
            other = r ^ (1 << bit)
            if r < other:
                small, large = jnp.minimum(rows[r], rows[other]), jnp.maximum(rows[r], rows[other])
                if down_bit is not None and (r >> down_bit) & 1:
                    small, large = large, small
                new[r], new[other] = small, large
        return new

    def exchange_sublanes(rows, distance):
        low = (sub & distance) == 0
        new = []
        for x in rows:
            y = swap_sublanes(x[None], distance)[0]
            new.append(jnp.where(low, jnp.minimum(x, y), jnp.maximum(x, y)))
        return new

    for stage in (1, 2, 3):
        for bit in range(stage - 1, -1, -1):
            rows = exchange(rows, bit, stage)
    for stage in (4, 5, 6, 7):
        flip = None
        if stage < 7:
            flip = jnp.where((sub & (1 << (stage - 4))) == 0, 1.0, -1.0)
            rows = [x * flip for x in rows]
        for bit in range(stage - 1, -1, -1):
            rows = exchange(rows, bit, None) if bit < 4 else exchange_sublanes(rows, 1 << (bit - 4))
        if flip is not None:
            rows = [x * flip for x in rows]
    return jnp.concatenate(rows, axis=0)


def partner_codes(order, info):
    taken = info > -0.5
    turns = jnp.maximum(info, 0.0)
    first, second = order[:PAIRS], order[PAIRS:]
    partner = jnp.concatenate([jnp.where(taken, second, first), jnp.where(taken, first, second)], axis=0)
    eighth = jnp.floor(order * 0.125)
    place = order * 16.0 - eighth * 127.0
    extra = jnp.concatenate([turns * 2.0, turns * 2.0 + 1.0], axis=0)
    return sort_rows(place * 65536.0 + partner * 512.0 + extra)


def collide(velocity, codes):
    partner = (codes >> 9) & 127
    turns = ((codes >> 1) & 255).astype(jnp.float32)
    other = [jnp.take_along_axis(v, partner, axis=1) for v in velocity]
    relative = [v - o for v, o in zip(velocity, other)]
    speed = jnp.sqrt(relative[0] * relative[0] + relative[1] * relative[1] + relative[2] * relative[2])
    half = 0.5 * speed
    half = jnp.where((codes & 1) == 0, half, -half)
    return [0.5 * (v + o) + half * u for v, o, u in zip(velocity, other, directions(turns))]


def split(x):
    high = x.astype(jnp.bfloat16)
    return high, (x - high.astype(jnp.float32)).astype(jnp.bfloat16)


def dot(a, b):
    return jnp.dot(a, b, preferred_element_type=jnp.float32)


def dot_lanes(a, b):
    return lax.dot_general(a, b, CONTRACT_LANES, preferred_element_type=jnp.float32)


def pick(selection, x):
    high, low = split(x)
    return dot(selection, high) + dot(selection, low)


def mover_selection(destination):
    up = destination == neighbour(1)
    down = destination == neighbour(-1)
    ahead = lax.broadcasted_iota(jnp.int32, (CAP, CAP), 0) < lax.broadcasted_iota(jnp.int32, (CAP, CAP), 1)
    flags = jnp.concatenate([jnp.where(up, 1.0, 0.0), jnp.where(down, 1.0, 0.0), jnp.zeros((6, CAP), jnp.float32)], axis=0)
    ranking = dot(flags.astype(jnp.bfloat16), jnp.where(ahead, 1.0, 0.0).astype(jnp.bfloat16))
    rows = lax.broadcasted_iota(jnp.int32, (MOVE, CAP), 0).astype(jnp.float32)
    chosen = [rows == jnp.where(moving, ranking[i : i + 1], -1.0) for i, moving in enumerate((up, down))]
    return jnp.where(jnp.concatenate(chosen, axis=0), 1.0, 0.0).astype(jnp.bfloat16)


def place_on_mesh():
    return lax.axis_index("space"), lax.axis_index("rep")


def neighbour(steps):
    slab, _ = place_on_mesh()
    return lax.rem(slab + SLABS + steps, SLABS)


def position_kernel(
    destination, order, accepted, direction, particles, cell, up, down, selected, targets, orders, takens, turns, data, cells, sems
):
    copies = [
        pltpu.make_async_copy(source, target, sems.at[i])
        for i, (source, target) in enumerate(
            (
                (destination, targets),
                (particles.at[0:3], data.at[0:3]),
                (order, orders),
                (accepted, takens),
                (direction, turns),
                (particles.at[3:6], data.at[3:6]),
                (cell, cells),
            )
        )
    ]
    for c in copies:
        c.start()
    copies[0].wait()
    selection = mover_selection(targets[...])
    selected[...] = selection
    copies[1].wait()
    for c in range(3):
        position = pick(selection, data[c, 0])
        up[c] = position[:MOVE]
        down[c] = position[MOVE:]
    for c in copies[2:]:
        c.wait()


def velocity_kernel(selected, orders, takens, turns, data, up, down):
    selection = selected[...]
    info = jnp.where(takens[0] == 1, turns[0], -1).astype(jnp.float32).astype(jnp.bfloat16)
    chosen = dot_lanes(info, selection)
    order_rows = dot(selection, orders[0].astype(jnp.float32).astype(jnp.bfloat16))
    velocity = [pick(selection, data[3 + c, 0]) for c in range(3)]
    for i, out in enumerate((up, down)):
        part = slice(i * MOVE, (i + 1) * MOVE)
        codes = partner_codes(order_rows[part].T, chosen[:, part]).T.astype(jnp.int32)
        result = collide([v[part] for v in velocity], codes)
        for c in range(3):
            out[c] = result[c]


def own_kernel(live_count, destination, order, accepted, direction, particles, cells, sent, moved, mine, theirs, out, sems):
    del sent
    slab, rep = place_on_mesh()
    live = lax.broadcasted_iota(jnp.int32, (1, CAP), 1) < live_count[0, 0]
    staying = jnp.where(live & (destination[...] == slab), 8388608.0, 0.0)
    cell = jnp.where(live, (cells[...] + rep * (CELLS // 2)) & (CELLS - 1), -1)
    ones = jnp.ones((8, PART), jnp.bfloat16)
    total = jnp.zeros((8, CELLS), jnp.float32)
    copies = []
    for i in range(CAP // PART):
        part = slice(i * PART, (i + 1) * PART)
        info = jnp.where(accepted[0, :, part] == 1, direction[0, :, part], -1).astype(jnp.float32)
        codes = partner_codes(order[0, part].astype(jnp.float32).T, info) + staying[:, part]
        codes = codes.T.astype(jnp.int32)
        keep = (codes >> 23) == 1
        result = collide([particles[3 + c, 0, part] for c in range(3)], codes)
        for c in range(3):
            out[3 + c, part] = jnp.where(keep, result[c], 0.0)
            out[c, part] = jnp.where(keep, particles[c, 0, part] + time_step * result[c], 0.0)
        copies.append(
            pltpu.make_async_copy(
                out.at[:, part], moved.at[:, 0, MOVE + i * PART : MOVE + (i + 1) * PART], sems.at[i]
            )
        )
        copies[i].start()
        onehot = lax.broadcasted_iota(jnp.int32, (CELLS, PART), 0) == cell[:, part]
        onehot = jnp.where(onehot, 1.0, 0.0).astype(jnp.bfloat16)
        squares = result[0] * result[0] + result[1] * result[1] + result[2] * result[2]
        sums = []
        for value in [*result, squares]:
            high, low = split(value)
            sums.append((dot_lanes(ones, high) + dot_lanes(ones, low))[:1])
        high, low = split(jnp.concatenate(sums + [jnp.zeros((4, PART), jnp.float32)], axis=0))
        total += dot_lanes(high, onehot) + dot_lanes(low, onehot)
    mine[...] = total[:4, : CELLS // 2]
    theirs[...] = total[:4, CELLS // 2 :]
    for c in copies:
        c.wait()


def arrivals_kernel(
    parts, held, velocity_below, velocity_above, position_below, position_above, mine, arrived, moved, samples, sums, place, sems
):
    del held
    copies = []
    ends = ((0, position_below, velocity_below), (MOVE + CAP, position_above, velocity_above))
    for i, (at, position, velocity) in enumerate(ends):
        copies.append(pltpu.make_async_copy(velocity, moved.at[3:6, 0, at : at + MOVE], sems.at[2 * i]))
        copies[-1].start()
    for i, (at, position, velocity) in enumerate(ends):
        for c in range(3):
            place[i, c] = position[c] + time_step * velocity[c]
        copies.append(pltpu.make_async_copy(place.at[i], moved.at[0:3, 0, at : at + MOVE], sems.at[2 * i + 1]))
        copies[-1].start()
    sums[:, 0] = (mine[...] + arrived[...]) * (1.0 / (PART * parts))
    copies.append(pltpu.make_async_copy(sums, samples, sems.at[4]))
    copies[-1].start()
    for c in copies:
        c.wait()


def whole(shape, at=None):
    at = at or (0,) * len(shape)
    return pl.BlockSpec(shape, lambda *_: at)


SMEM = pl.BlockSpec(memory_space=pltpu.SMEM)
VMEM = pl.BlockSpec(memory_space=pltpu.VMEM)
HBM = pl.BlockSpec(memory_space=pltpu.HBM)


def in_hbm(*arrays):
    return [pltpu.with_memory_space_constraint(a, pltpu.HBM) for a in arrays]


def from_behind(value, axis, steps):
    count = lax.axis_size(axis)
    pairs = [(source, (source + steps) % count) for source in range(count)]
    return lax.ppermute(value, axis, pairs)


def per_device(particles, pair_order, accepted, direction, destination, live_count, cell_index):
    accepted = jnp.swapaxes(accepted, 1, 2)
    direction = jnp.swapaxes(direction, 1, 2)
    parts = lax.axis_size("rep")
    f32 = jnp.float32
    limit = pltpu.CompilerParams(vmem_limit_bytes=32 * 2**20)

    sent = jax.ShapeDtypeStruct((3, MOVE, PART), f32)
    up_position, down_position, selected, targets, orders, takens, turns, data, cells = pl.pallas_call(
        position_kernel,
        in_specs=[HBM] * 6,
        out_specs=[VMEM] * 9,
        out_shape=[
            sent,
            sent,
            pltpu.VMEM((2 * MOVE, CAP), jnp.bfloat16),
            pltpu.VMEM((1, CAP), jnp.int32),
            pltpu.VMEM((1, CAP, PART), jnp.int32),
            pltpu.VMEM((1, PAIRS, CAP), jnp.int32),
            pltpu.VMEM((1, PAIRS, CAP), jnp.int32),
            pltpu.VMEM((6, 1, CAP, PART), f32),
            pltpu.VMEM((1, CAP), jnp.int32),
        ],
        scratch_shapes=[pltpu.SemaphoreType.DMA((7,))],
        compiler_params=limit,
    )(*in_hbm(destination, pair_order, accepted, direction, particles, cell_index))
    position_below = from_behind(up_position, "space", 1)
    position_above = from_behind(down_position, "space", -1)
    up_velocity, down_velocity = pl.pallas_call(
        velocity_kernel,
        in_specs=[VMEM] * 5,
        out_specs=[VMEM] * 2,
        out_shape=[sent, sent],
        compiler_params=limit,
    )(selected, orders, takens, turns, data)
    velocity_below = from_behind(up_velocity, "space", 1)
    velocity_above = from_behind(down_velocity, "space", -1)
    held = (targets, orders, takens, turns, data, cells)

    half = jax.ShapeDtypeStruct((4, CELLS // 2), f32)
    moved, mine, theirs = pl.pallas_call(
        own_kernel,
        in_specs=[SMEM] + [VMEM] * 6 + [HBM],
        out_specs=[HBM, VMEM, VMEM],
        out_shape=[jax.ShapeDtypeStruct((6, 1, OUTCAP, PART), f32), half, half],
        scratch_shapes=[pltpu.VMEM((6, CAP, PART), f32), pltpu.SemaphoreType.DMA((CAP // PART,))],
        compiler_params=limit,
    )(live_count, *held, down_velocity)
    arrived = from_behind(theirs, "rep", 1)
    moved, samples = pl.pallas_call(
        functools.partial(arrivals_kernel, parts),
        in_specs=[HBM] + [VMEM] * 6,
        out_specs=[HBM, HBM],
        out_shape=[jax.ShapeDtypeStruct(moved.shape, f32), jax.ShapeDtypeStruct((4, 1, CELLS // 2), f32)],
        input_output_aliases={0: 0},
        scratch_shapes=[pltpu.VMEM((4, 1, CELLS // 2), f32), pltpu.VMEM((2, 3, MOVE, PART), f32), pltpu.SemaphoreType.DMA((5,))],
        compiler_params=pltpu.CompilerParams(vmem_limit_bytes=8 * 2**20),
    )(moved, velocity_below, velocity_above, position_below, position_above, mine, arrived)
    return (moved, samples)


def solution(mesh):
    return jax.shard_map(
        per_device,
        mesh=mesh,
        in_specs=(
            P(None, "rep", "space", None),
            P("rep", "space", None),
            P("rep", "space", None),
            P("rep", "space", None),
            P("rep", "space"),
            P("rep", "space"),
            P("rep", "space"),
        ),
        out_specs=(P(None, "rep", "space", None), P(None, "space", "rep")),
        check_vma=False,
    )
```

```python
import functools

import jax
import jax.numpy as jnp
import numpy as np
from jax import lax
from jax.experimental import pallas as pl
from jax.experimental.pallas import tpu as pltpu
from jax.sharding import PartitionSpec as P

PART = 128
PAIRS = 64
NDIR = 256
CAP = 512
MOVE = 128
CELLS = 256
OUTCAP = 768
SLABS = 64

time_step = 0.25
golden_turn = 2.399963229728653
TURN_HIGH = float(np.round(golden_turn / (2 * np.pi) * 4096) / 4096)
TURN_LOW = float(golden_turn / (2 * np.pi) - TURN_HIGH)

CONTRACT_LANES = (((1,), (1,)), ((), ()))


def fitted(function, powers):
    x = 0.25 * np.cos((np.arange(400) + 0.5) * np.pi / 400)
    basis = np.stack([x**p for p in powers], axis=1)
    return [float(c) for c in np.linalg.lstsq(basis, function(x), rcond=None)[0]]


SINE = fitted(lambda x: np.sin(2 * np.pi * x), [1, 3, 5, 7, 9])
COSINE = fitted(lambda x: np.cos(2 * np.pi * x), [0, 2, 4, 6, 8])


def polynomial(x, coefficients):
    total = jnp.full_like(x, coefficients[-1])
    for c in coefficients[-2::-1]:
        total = total * x + c
    return total


def directions(turns):
    height = 1.0 - (2.0 * turns + 1.0) * (1.0 / NDIR)
    radius = jnp.sqrt(1.0 - height * height)
    whole = turns * TURN_HIGH
    part = (whole - jnp.floor(whole + 0.5)) + turns * TURN_LOW
    fold = jnp.abs(part) - 0.25
    square = fold * fold
    cosine = -fold * polynomial(square, SINE)
    sine = polynomial(square, COSINE)
    sine = jnp.where(part < 0.0, -sine, sine)
    return radius * cosine, radius * sine, height


def swap_sublanes(x, distance):
    return jnp.take_along_axis(x, lax.broadcasted_iota(jnp.int32, x.shape, 0) ^ distance, axis=0)


def sort_rows(keys):
    n = keys.shape[-1]
    rows = [keys[8 * r : 8 * r + 8] for r in range(16)]
    sub = lax.broadcasted_iota(jnp.int32, (8, n), 0)

    def exchange(rows, bit, down_bit):
        new = list(rows)
        for r in range(16):
            other = r ^ (1 << bit)
            if r < other:
                small, large = jnp.minimum(rows[r], rows[other]), jnp.maximum(rows[r], rows[other])
                if down_bit is not None and (r >> down_bit) & 1:
                    small, large = large, small
                new[r], new[other] = small, large
        return new

    def exchange_sublanes(rows, distance):
        low = (sub & distance) == 0
        new = []
        for x in rows:
            y = swap_sublanes(x, distance)
            new.append(jnp.where(low, jnp.minimum(x, y), jnp.maximum(x, y)))
        return new

    for stage in (1, 2, 3):
        for bit in range(stage - 1, -1, -1):
            rows = exchange(rows, bit, stage)
    for stage in (4, 5, 6, 7):
        flip = None
        if stage < 7:
            flip = jnp.where((sub & (1 << (stage - 4))) == 0, 1.0, -1.0)
            rows = [x * flip for x in rows]
        for bit in range(stage - 1, -1, -1):
            rows = exchange(rows, bit, None) if bit < 4 else exchange_sublanes(rows, 1 << (bit - 4))
        if flip is not None:
            rows = [x * flip for x in rows]
    return jnp.concatenate(rows, axis=0)


def partner_codes(order, info):
    taken = info > -0.5
    turns = jnp.maximum(info, 0.0)
    first, second = order[:PAIRS], order[PAIRS:]
    partner = jnp.concatenate([jnp.where(taken, second, first), jnp.where(taken, first, second)], axis=0)
    eighth = jnp.floor(order * 0.125)
    place = order * 16.0 - eighth * 127.0
    extra = jnp.concatenate([turns * 2.0, turns * 2.0 + 1.0], axis=0)
    return sort_rows(place * 65536.0 + partner * 512.0 + extra)


def collide(velocity, codes):
    partner = (codes >> 9) & 127
    turns = ((codes >> 1) & 255).astype(jnp.float32)
    other = [jnp.take_along_axis(v, partner, axis=1) for v in velocity]
    relative = [v - o for v, o in zip(velocity, other)]
    speed = jnp.sqrt(relative[0] * relative[0] + relative[1] * relative[1] + relative[2] * relative[2])
    half = 0.5 * speed
    half = jnp.where((codes & 1) == 0, half, -half)
    return [0.5 * (v + o) + half * u for v, o, u in zip(velocity, other, directions(turns))]


def split(x):
    high = x.astype(jnp.bfloat16)
    return high, (x - high.astype(jnp.float32)).astype(jnp.bfloat16)


def dot(a, b):
    return jnp.dot(a, b, preferred_element_type=jnp.float32)


def dot_lanes(a, b):
    return lax.dot_general(a, b, CONTRACT_LANES, preferred_element_type=jnp.float32)


def pick(selection, x):
    both = dot(selection, jnp.concatenate(split(x), axis=1))
    return both[:, :PART] + both[:, PART:]


def mover_selection(destination):
    up = destination == neighbour(1)
    down = destination == neighbour(-1)
    pieces = CAP // PART
    flags = jnp.concatenate(
        [jnp.where(m[:, i * PART : (i + 1) * PART], 1.0, 0.0) for m in (up, down) for i in range(pieces)], axis=0
    )
    ahead = lax.broadcasted_iota(jnp.int32, (PART, 2 * PART), 0) < lax.broadcasted_iota(jnp.int32, (PART, 2 * PART), 1)
    counts = dot(flags.astype(jnp.bfloat16), jnp.where(ahead, 1.0, 0.0).astype(jnp.bfloat16))
    rows = lax.broadcasted_iota(jnp.int32, (MOVE, PART), 0).astype(jnp.float32)
    chosen = []
    for d in range(2):
        parts, before = [], jnp.zeros((1, PART), jnp.float32)
        for i in range(pieces):
            at = pieces * d + i
            ranking = jnp.where(flags[at : at + 1] > 0.5, counts[at : at + 1, :PART] + before, -1.0)
            before += counts[at : at + 1, PART:]
            parts.append(jnp.where(rows == ranking, 1.0, 0.0).astype(jnp.bfloat16))
        chosen.append(jnp.concatenate(parts, axis=1))
    return jnp.concatenate(chosen, axis=0)


def place_on_mesh():
    return lax.axis_index("space"), lax.axis_index("rep")


def neighbour(steps):
    slab, _ = place_on_mesh()
    return lax.rem(slab + SLABS + steps, SLABS)


def movers_kernel(
    destination, order, accepted, direction, particles, cell, up, down, targets, orders, takens, turns, data, cells, sems
):
    copies = [
        pltpu.make_async_copy(source, target, sems.at[i])
        for i, (source, target) in enumerate(
            (
                (destination, targets),
                (particles.at[3:6], data.at[3:6]),
                (order, orders),
                (accepted, takens),
                (direction, turns),
                (particles.at[0:3], data.at[0:3]),
                (cell, cells),
            )
        )
    ]
    for c in copies:
        c.start()
    copies[0].wait()
    selection = mover_selection(targets[...])
    copies[1].wait()
    velocity = [pick(selection, data[3 + c, 0]) for c in range(3)]
    for c in copies[2:]:
        c.wait()
    info = jnp.where(takens[0] == 1, turns[0], -1).astype(jnp.float32).astype(jnp.bfloat16)
    chosen = dot_lanes(info, selection)
    order_rows = dot(selection, orders[0].astype(jnp.float32).astype(jnp.bfloat16))
    position = [pick(selection, data[c, 0]) for c in range(3)]
    codes = []
    for i in range(2):
        part = slice(i * MOVE, (i + 1) * MOVE)
        codes.append(partner_codes(order_rows[part].T, chosen[:, part]).T.astype(jnp.int32))
    for i, out in enumerate((up, down)):
        part = slice(i * MOVE, (i + 1) * MOVE)
        result = collide([v[part] for v in velocity], codes[i])
        for c in range(3):
            out[3 + c] = result[c]
            out[c] = position[c][part] + time_step * result[c]


def own_kernel(live_count, destination, order, accepted, direction, particles, cells, moved, mine, theirs, out, sems):
    slab, rep = place_on_mesh()
    live = lax.broadcasted_iota(jnp.int32, (1, CAP), 1) < live_count[0, 0]
    staying = jnp.where(live & (destination[...] == slab), 8388608.0, 0.0)
    cell = jnp.where(live, (cells[...] + rep * (CELLS // 2)) & (CELLS - 1), -1)
    ones = jnp.ones((8, PART), jnp.bfloat16)
    total = jnp.zeros((8, CELLS), jnp.float32)
    copies = []
    for i in range(CAP // PART):
        part = slice(i * PART, (i + 1) * PART)
        info = jnp.where(accepted[0, :, part] == 1, direction[0, :, part], -1).astype(jnp.float32)
        codes = partner_codes(order[0, part].astype(jnp.float32).T, info) + staying[:, part]
        codes = codes.T.astype(jnp.int32)
        keep = (codes >> 23) == 1
        result = collide([particles[3 + c, 0, part] for c in range(3)], codes)
        for c in range(3):
            out[3 + c, part] = jnp.where(keep, result[c], 0.0)
            out[c, part] = jnp.where(keep, particles[c, 0, part] + time_step * result[c], 0.0)
        copies.append(
            pltpu.make_async_copy(
                out.at[:, part], moved.at[:, 0, MOVE + i * PART : MOVE + (i + 1) * PART], sems.at[i]
            )
        )
        copies[i].start()
        onehot = lax.broadcasted_iota(jnp.int32, (CELLS, PART), 0) == cell[:, part]
        onehot = jnp.where(onehot, 1.0, 0.0).astype(jnp.bfloat16)
        squares = result[0] * result[0] + result[1] * result[1] + result[2] * result[2]
        sums = []
        for value in [*result, squares]:
            high, low = split(value)
            sums.append((dot_lanes(ones, high) + dot_lanes(ones, low))[:1])
        high, low = split(jnp.concatenate(sums + [jnp.zeros((4, PART), jnp.float32)], axis=0))
        total += dot_lanes(high, onehot) + dot_lanes(low, onehot)
    mine[...] = total[:4, : CELLS // 2]
    theirs[...] = total[:4, CELLS // 2 :]
    for c in copies:
        c.wait()


def arrivals_kernel(parts, held, below, above, mine, arrived, moved, samples, sums, sems):
    del held
    copies = [
        pltpu.make_async_copy(below, moved.at[:, 0, 0:MOVE], sems.at[0]),
        pltpu.make_async_copy(above, moved.at[:, 0, MOVE + CAP : OUTCAP], sems.at[1]),
        pltpu.make_async_copy(sums, samples, sems.at[2]),
    ]
    copies[0].start()
    copies[1].start()
    sums[:, 0] = (mine[...] + arrived[...]) * (1.0 / (PART * parts))
    copies[2].start()
    for c in copies:
        c.wait()


def whole(shape, at=None):
    at = at or (0,) * len(shape)
    return pl.BlockSpec(shape, lambda *_: at)


SMEM = pl.BlockSpec(memory_space=pltpu.SMEM)
VMEM = pl.BlockSpec(memory_space=pltpu.VMEM)
HBM = pl.BlockSpec(memory_space=pltpu.HBM)


def in_hbm(*arrays):
    return [pltpu.with_memory_space_constraint(a, pltpu.HBM) for a in arrays]


def from_behind(value, axis, steps):
    count = lax.axis_size(axis)
    pairs = [(source, (source + steps) % count) for source in range(count)]
    return lax.ppermute(value, axis, pairs)


def per_device(particles, pair_order, accepted, direction, destination, live_count, cell_index):
    accepted = jnp.swapaxes(accepted, 1, 2)
    direction = jnp.swapaxes(direction, 1, 2)
    parts = lax.axis_size("rep")
    f32 = jnp.float32
    limit = pltpu.CompilerParams(vmem_limit_bytes=32 * 2**20)

    sent = jax.ShapeDtypeStruct((6, MOVE, PART), f32)
    up, down, *held = pl.pallas_call(
        movers_kernel,
        in_specs=[HBM] * 6,
        out_specs=[VMEM] * 8,
        out_shape=[
            sent,
            sent,
            pltpu.VMEM((1, CAP), jnp.int32),
            pltpu.VMEM((1, CAP, PART), jnp.int32),
            pltpu.VMEM((1, PAIRS, CAP), jnp.int32),
            pltpu.VMEM((1, PAIRS, CAP), jnp.int32),
            pltpu.VMEM((6, 1, CAP, PART), f32),
            pltpu.VMEM((1, CAP), jnp.int32),
        ],
        scratch_shapes=[pltpu.SemaphoreType.DMA((7,))],
        compiler_params=limit,
    )(*in_hbm(destination, pair_order, accepted, direction, particles, cell_index))
    from_lower = from_behind(up, "space", 1)
    from_upper = from_behind(down, "space", -1)

    half = jax.ShapeDtypeStruct((4, CELLS // 2), f32)
    moved, mine, theirs = pl.pallas_call(
        own_kernel,
        in_specs=[SMEM] + [VMEM] * 6,
        out_specs=[HBM, VMEM, VMEM],
        out_shape=[jax.ShapeDtypeStruct((6, 1, OUTCAP, PART), f32), half, half],
        scratch_shapes=[pltpu.VMEM((6, CAP, PART), f32), pltpu.SemaphoreType.DMA((CAP // PART,))],
        compiler_params=limit,
    )(live_count, *held)
    arrived = from_behind(theirs, "rep", 1)
    moved, samples = pl.pallas_call(
        functools.partial(arrivals_kernel, parts),
        in_specs=[HBM, VMEM, VMEM, VMEM, VMEM],
        out_specs=[HBM, HBM],
        out_shape=[jax.ShapeDtypeStruct(moved.shape, f32), jax.ShapeDtypeStruct((4, 1, CELLS // 2), f32)],
        input_output_aliases={0: 0},
        scratch_shapes=[pltpu.VMEM((4, 1, CELLS // 2), f32), pltpu.SemaphoreType.DMA((3,))],
        compiler_params=pltpu.CompilerParams(vmem_limit_bytes=8 * 2**20),
    )(moved, from_lower, from_upper, mine, arrived)
    return (moved, samples)


def solution(mesh):
    return jax.shard_map(
        per_device,
        mesh=mesh,
        in_specs=(
            P(None, "rep", "space", None),
            P("rep", "space", None),
            P("rep", "space", None),
            P("rep", "space", None),
            P("rep", "space"),
            P("rep", "space"),
            P("rep", "space"),
        ),
        out_specs=(P(None, "rep", "space", None), P(None, "space", "rep")),
        check_vma=False,
    )
```

```python
import functools

import jax
import jax.numpy as jnp
import numpy as np
from jax import lax
from jax.experimental import pallas as pl
from jax.experimental.pallas import tpu as pltpu
from jax.sharding import PartitionSpec as P

PART = 128
PAIRS = 64
NDIR = 256
CAP = 512
MOVE = 128
CELLS = 256
OUTCAP = 768
SLABS = 64

time_step = 0.25
golden_turn = 2.399963229728653
TURN_HIGH = float(np.round(golden_turn / (2 * np.pi) * 4096) / 4096)
TURN_LOW = float(golden_turn / (2 * np.pi) - TURN_HIGH)

CONTRACT_LANES = (((1,), (1,)), ((), ()))


def fitted(function, powers):
    x = 0.25 * np.cos((np.arange(400) + 0.5) * np.pi / 400)
    basis = np.stack([x**p for p in powers], axis=1)
    return [float(c) for c in np.linalg.lstsq(basis, function(x), rcond=None)[0]]


SINE = fitted(lambda x: np.sin(2 * np.pi * x), [1, 3, 5, 7, 9])
COSINE = fitted(lambda x: np.cos(2 * np.pi * x), [0, 2, 4, 6, 8])


def polynomial(x, coefficients):
    total = jnp.full_like(x, coefficients[-1])
    for c in coefficients[-2::-1]:
        total = total * x + c
    return total


def directions(turns):
    height = 1.0 - (2.0 * turns + 1.0) * (1.0 / NDIR)
    radius = jnp.sqrt(1.0 - height * height)
    whole = turns * TURN_HIGH
    part = (whole - jnp.floor(whole + 0.5)) + turns * TURN_LOW
    fold = jnp.abs(part) - 0.25
    square = fold * fold
    cosine = -fold * polynomial(square, SINE)
    sine = polynomial(square, COSINE)
    sine = jnp.where(part < 0.0, -sine, sine)
    return radius * cosine, radius * sine, height


def swap_sublanes(x, distance):
    return jnp.take_along_axis(x, lax.broadcasted_iota(jnp.int32, x.shape, 0) ^ distance, axis=0)


def sort_rows(keys):
    n = keys.shape[-1]
    rows = [keys[8 * r : 8 * r + 8] for r in range(16)]
    sub = lax.broadcasted_iota(jnp.int32, (8, n), 0)

    def exchange(rows, bit, down_bit):
        new = list(rows)
        for r in range(16):
            other = r ^ (1 << bit)
            if r < other:
                small, large = jnp.minimum(rows[r], rows[other]), jnp.maximum(rows[r], rows[other])
                if down_bit is not None and (r >> down_bit) & 1:
                    small, large = large, small
                new[r], new[other] = small, large
        return new

    def exchange_sublanes(rows, distance):
        low = (sub & distance) == 0
        new = []
        for x in rows:
            y = swap_sublanes(x, distance)
            new.append(jnp.where(low, jnp.minimum(x, y), jnp.maximum(x, y)))
        return new

    for stage in (1, 2, 3):
        for bit in range(stage - 1, -1, -1):
            rows = exchange(rows, bit, stage)
    for stage in (4, 5, 6, 7):
        flip = None
        if stage < 7:
            flip = jnp.where((sub & (1 << (stage - 4))) == 0, 1.0, -1.0)
            rows = [x * flip for x in rows]
        for bit in range(stage - 1, -1, -1):
            rows = exchange(rows, bit, None) if bit < 4 else exchange_sublanes(rows, 1 << (bit - 4))
        if flip is not None:
            rows = [x * flip for x in rows]
    return jnp.concatenate(rows, axis=0)


def partner_codes(order, info):
    taken = info > -0.5
    turns = jnp.maximum(info, 0.0)
    first, second = order[:PAIRS], order[PAIRS:]
    partner = jnp.concatenate([jnp.where(taken, second, first), jnp.where(taken, first, second)], axis=0)
    eighth = jnp.floor(order * 0.125)
    place = order * 16.0 - eighth * 127.0
    extra = jnp.concatenate([turns * 2.0, turns * 2.0 + 1.0], axis=0)
    return sort_rows(place * 65536.0 + partner * 512.0 + extra)


def collide(velocity, codes):
    partner = (codes >> 9) & 127
    turns = ((codes >> 1) & 255).astype(jnp.float32)
    other = [jnp.take_along_axis(v, partner, axis=1) for v in velocity]
    relative = [v - o for v, o in zip(velocity, other)]
    speed = jnp.sqrt(relative[0] * relative[0] + relative[1] * relative[1] + relative[2] * relative[2])
    half = 0.5 * speed
    half = jnp.where((codes & 1) == 0, half, -half)
    return [0.5 * (v + o) + half * u for v, o, u in zip(velocity, other, directions(turns))]


def split(x):
    high = x.astype(jnp.bfloat16)
    return high, (x - high.astype(jnp.float32)).astype(jnp.bfloat16)


def dot(a, b):
    return jnp.dot(a, b, preferred_element_type=jnp.float32)


def dot_lanes(a, b):
    return lax.dot_general(a, b, CONTRACT_LANES, preferred_element_type=jnp.float32)


def pick(selection, x):
    both = dot(selection, jnp.concatenate(split(x), axis=1))
    return both[:, :PART] + both[:, PART:]


def mover_selection(destination):
    up = destination == neighbour(1)
    down = destination == neighbour(-1)
    pieces = CAP // PART
    flags = jnp.concatenate(
        [jnp.where(m[:, i * PART : (i + 1) * PART], 1.0, 0.0) for m in (up, down) for i in range(pieces)], axis=0
    )
    ahead = lax.broadcasted_iota(jnp.int32, (PART, 2 * PART), 0) < lax.broadcasted_iota(jnp.int32, (PART, 2 * PART), 1)
    counts = dot(flags.astype(jnp.bfloat16), jnp.where(ahead, 1.0, 0.0).astype(jnp.bfloat16))
    rows = lax.broadcasted_iota(jnp.int32, (MOVE, PART), 0).astype(jnp.float32)
    chosen = []
    for d in range(2):
        parts, before = [], jnp.zeros((1, PART), jnp.float32)
        for i in range(pieces):
            at = pieces * d + i
            ranking = jnp.where(flags[at : at + 1] > 0.5, counts[at : at + 1, :PART] + before, -1.0)
            before += counts[at : at + 1, PART:]
            parts.append(jnp.where(rows == ranking, 1.0, 0.0).astype(jnp.bfloat16))
        chosen.append(jnp.concatenate(parts, axis=1))
    return jnp.concatenate(chosen, axis=0)


def place_on_mesh():
    return lax.axis_index("space"), lax.axis_index("rep")


def neighbour(steps):
    slab, _ = place_on_mesh()
    return lax.rem(slab + SLABS + steps, SLABS)


def movers_kernel(
    destination, order, accepted, direction, particles, cell, up, down, targets, orders, takens, turns, data, cells, sems
):
    copies = [
        pltpu.make_async_copy(source, target, sems.at[i])
        for i, (source, target) in enumerate(
            (
                (destination, targets),
                (order, orders),
                (accepted, takens),
                (direction, turns),
                (particles, data),
                (cell, cells),
            )
        )
    ]
    for c in copies:
        c.start()
    copies[0].wait()
    selection = mover_selection(targets[...])
    for c in copies[1:4]:
        c.wait()
    info = jnp.where(takens[0] == 1, turns[0], -1).astype(jnp.float32).astype(jnp.bfloat16)
    flipped = orders[0].astype(jnp.float32).T.astype(jnp.bfloat16)
    picked = dot_lanes(jnp.concatenate([flipped, info], axis=0), selection)
    codes = []
    for i in range(2):
        part = slice(i * MOVE, (i + 1) * MOVE)
        codes.append(partner_codes(picked[:PART, part], picked[PART:, part]).T.astype(jnp.int32))
    copies[4].wait()
    velocity = [pick(selection, data[3 + c, 0]) for c in range(3)]
    position = [pick(selection, data[c, 0]) for c in range(3)]
    for i, out in enumerate((up, down)):
        part = slice(i * MOVE, (i + 1) * MOVE)
        result = collide([v[part] for v in velocity], codes[i])
        for c in range(3):
            out[3 + c] = result[c]
            out[c] = position[c][part] + time_step * result[c]
    copies[5].wait()


def own_kernel(live_count, destination, order, accepted, direction, particles, cells, moved, mine, theirs, out, sems):
    slab, rep = place_on_mesh()
    live = lax.broadcasted_iota(jnp.int32, (1, CAP), 1) < live_count[0, 0]
    staying = jnp.where(live & (destination[...] == slab), 8388608.0, 0.0)
    cell = jnp.where(live, (cells[...] + rep * (CELLS // 2)) & (CELLS - 1), -1)
    ones = jnp.ones((8, PART), jnp.bfloat16)
    total = jnp.zeros((8, CELLS), jnp.float32)
    copies = []
    for i in range(CAP // PART):
        part = slice(i * PART, (i + 1) * PART)
        info = jnp.where(accepted[0, :, part] == 1, direction[0, :, part], -1).astype(jnp.float32)
        codes = partner_codes(order[0, part].astype(jnp.float32).T, info) + staying[:, part]
        codes = codes.T.astype(jnp.int32)
        keep = (codes >> 23) == 1
        result = collide([particles[3 + c, 0, part] for c in range(3)], codes)
        for c in range(3):
            out[3 + c, part] = jnp.where(keep, result[c], 0.0)
            out[c, part] = jnp.where(keep, particles[c, 0, part] + time_step * result[c], 0.0)
        copies.append(
            pltpu.make_async_copy(
                out.at[:, part], moved.at[:, 0, MOVE + i * PART : MOVE + (i + 1) * PART], sems.at[i]
            )
        )
        copies[i].start()
        onehot = lax.broadcasted_iota(jnp.int32, (CELLS, PART), 0) == cell[:, part]
        onehot = jnp.where(onehot, 1.0, 0.0).astype(jnp.bfloat16)
        squares = result[0] * result[0] + result[1] * result[1] + result[2] * result[2]
        sums = []
        for value in [*result, squares]:
            high, low = split(value)
            sums.append((dot_lanes(ones, high) + dot_lanes(ones, low))[:1])
        high, low = split(jnp.concatenate(sums + [jnp.zeros((4, PART), jnp.float32)], axis=0))
        total += dot_lanes(high, onehot) + dot_lanes(low, onehot)
    mine[...] = total[:4, : CELLS // 2]
    theirs[...] = total[:4, CELLS // 2 :]
    for c in copies:
        c.wait()


def arrivals_kernel(parts, held, below, above, mine, arrived, moved, samples, sums, sems):
    del held
    copies = [
        pltpu.make_async_copy(below, moved.at[:, 0, 0:MOVE], sems.at[0]),
        pltpu.make_async_copy(above, moved.at[:, 0, MOVE + CAP : OUTCAP], sems.at[1]),
        pltpu.make_async_copy(sums, samples, sems.at[2]),
    ]
    copies[0].start()
    copies[1].start()
    sums[:, 0] = (mine[...] + arrived[...]) * (1.0 / (PART * parts))
    copies[2].start()
    for c in copies:
        c.wait()


def whole(shape, at=None):
    at = at or (0,) * len(shape)
    return pl.BlockSpec(shape, lambda *_: at)


SMEM = pl.BlockSpec(memory_space=pltpu.SMEM)
VMEM = pl.BlockSpec(memory_space=pltpu.VMEM)
HBM = pl.BlockSpec(memory_space=pltpu.HBM)


def in_hbm(*arrays):
    return [pltpu.with_memory_space_constraint(a, pltpu.HBM) for a in arrays]


def from_behind(value, axis, steps):
    count = lax.axis_size(axis)
    pairs = [(source, (source + steps) % count) for source in range(count)]
    return lax.ppermute(value, axis, pairs)


def per_device(particles, pair_order, accepted, direction, destination, live_count, cell_index):
    accepted = jnp.swapaxes(accepted, 1, 2)
    direction = jnp.swapaxes(direction, 1, 2)
    parts = lax.axis_size("rep")
    f32 = jnp.float32
    limit = pltpu.CompilerParams(vmem_limit_bytes=32 * 2**20)

    sent = jax.ShapeDtypeStruct((6, MOVE, PART), f32)
    up, down, *held = pl.pallas_call(
        movers_kernel,
        in_specs=[HBM] * 6,
        out_specs=[VMEM] * 8,
        out_shape=[
            sent,
            sent,
            pltpu.VMEM((1, CAP), jnp.int32),
            pltpu.VMEM((1, CAP, PART), jnp.int32),
            pltpu.VMEM((1, PAIRS, CAP), jnp.int32),
            pltpu.VMEM((1, PAIRS, CAP), jnp.int32),
            pltpu.VMEM((6, 1, CAP, PART), f32),
            pltpu.VMEM((1, CAP), jnp.int32),
        ],
        scratch_shapes=[pltpu.SemaphoreType.DMA((6,))],
        compiler_params=limit,
    )(*in_hbm(destination, pair_order, accepted, direction, particles, cell_index))
    from_lower = from_behind(up, "space", 1)
    from_upper = from_behind(down, "space", -1)

    half = jax.ShapeDtypeStruct((4, CELLS // 2), f32)
    moved, mine, theirs = pl.pallas_call(
        own_kernel,
        in_specs=[SMEM] + [VMEM] * 6,
        out_specs=[HBM, VMEM, VMEM],
        out_shape=[jax.ShapeDtypeStruct((6, 1, OUTCAP, PART), f32), half, half],
        scratch_shapes=[pltpu.VMEM((6, CAP, PART), f32), pltpu.SemaphoreType.DMA((CAP // PART,))],
        compiler_params=limit,
    )(live_count, *held)
    arrived = from_behind(theirs, "rep", 1)
    moved, samples = pl.pallas_call(
        functools.partial(arrivals_kernel, parts),
        in_specs=[HBM, VMEM, VMEM, VMEM, VMEM],
        out_specs=[HBM, HBM],
        out_shape=[jax.ShapeDtypeStruct(moved.shape, f32), jax.ShapeDtypeStruct((4, 1, CELLS // 2), f32)],
        input_output_aliases={0: 0},
        scratch_shapes=[pltpu.VMEM((4, 1, CELLS // 2), f32), pltpu.SemaphoreType.DMA((3,))],
        compiler_params=pltpu.CompilerParams(vmem_limit_bytes=8 * 2**20),
    )(moved, from_lower, from_upper, mine, arrived)
    return (moved, samples)


def solution(mesh):
    return jax.shard_map(
        per_device,
        mesh=mesh,
        in_specs=(
            P(None, "rep", "space", None),
            P("rep", "space", None),
            P("rep", "space", None),
            P("rep", "space", None),
            P("rep", "space"),
            P("rep", "space"),
            P("rep", "space"),
        ),
        out_specs=(P(None, "rep", "space", None), P(None, "space", "rep")),
        check_vma=False,
    )
```
